256 devices in a mesh: batch: 32 (over z, y), space: 8 (over x, core).
Axes of the slice: x: 4, y: 4, z: 8, core: 2. Of those that a mesh axis runs over, the one named last changes fastest.
Arguments:
- features: bfloat16 [32, 96, 72, 1024], P('batch', 'space'), may hold values from -600 to 600
- depth_one: bfloat16 [3, 3, 1024], replicated, may hold values from -2 to 2
- gain_one: float32 [1024], replicated, may hold values from 0.25 to 1.75
- shift_one: float32 [1024], replicated, may hold values from -3 to 3
- point_one: bfloat16 [1024, 1536], replicated, may hold values from -0.1875 to 0.1875
- gain_two: float32 [1536], replicated, may hold values from 0.25 to 1.75
- shift_two: float32 [1536], replicated, may hold values from -3 to 3
- depth_two: bfloat16 [3, 3, 1536], replicated, may hold values from -2 to 2
- gain_three: float32 [1536], replicated, may hold values from 0.25 to 1.75
- shift_three: float32 [1536], replicated, may hold values from -3 to 3
- point_two: bfloat16 [1536, 2048], replicated, may hold values from -0.15625 to 0.15625
- gain_four: float32 [2048], replicated, may hold values from 0.25 to 1.75
- shift_four: float32 [2048], replicated, may hold values from -3 to 3
Outputs:
- exit_map: bfloat16 [32, 96, 72, 2048], P('batch', 'space')
The draws below stay inside these ranges and needn't reach their ends.
All inputs are finite; a program needn't handle non-finite values.
Results may differ from the reference program's by a relative error of at most 0.0079.
Values may be sent and summed in bfloat16 or wider, within the bound.
No kernel may reach another device: no remote copies, remote signals or barrier semaphores. Data moves between devices by JAX's collectives and lax.ppermute only.
A program may use at most 64 MiB of HBM per device.

```python
import jax
import jax.numpy as jnp
from jax import lax

CH_IN = 1024
CH_MID = 1536
CH_OUT = 2048
COLS = 72
RATE = 2
LATS = 96
SAMPLES = 32


def draw_features(key, part):
    key_base, key_chan = jax.random.split(key, 2)
    sample_ramp = 3.0 ** (jnp.arange(SAMPLES, dtype=jnp.float32) / max(SAMPLES - 1, 1))
    row_ramp = 3.0 ** (jnp.arange(LATS, dtype=jnp.float32) / max(LATS - 1, 1))
    base = jnp.clip(jax.random.normal(key_base, (SAMPLES, LATS, COLS, CH_IN), jnp.float32), -6.0, 6.0)
    channel_scale = jax.random.uniform(key_chan, (CH_IN,), jnp.float32, 0.5, 2.0)
    values = base * sample_ramp[:, None, None, None] * row_ramp[None, :, None, None] * channel_scale
    return values.astype(jnp.bfloat16)


def bell_draw(stream_key, shape, deviation, limit, kind=jnp.bfloat16):
    entries = jax.random.normal(stream_key, shape, jnp.float32) * deviation
    return jnp.minimum(jnp.maximum(entries, -limit), limit).astype(kind)


def setup_inputs(seed: int = 0) -> dict:
    seeds = jax.random.split(jax.random.key(seed), 14)
    features = draw_features(jax.random.fold_in(seeds[13], 71), 0)
    depth_one = bell_draw(seeds[1], (3, 3, CH_IN), 9 ** -0.5, 2.0)
    gain_one = jnp.clip(1.0 + 0.15 * jax.random.normal(seeds[2], (CH_IN,), jnp.float32), 0.25, 1.75)
    shift_one = bell_draw(seeds[3], (CH_IN,), 0.5, 3.0, jnp.float32)
    point_one = bell_draw(seeds[4], (CH_IN, CH_MID), CH_IN ** -0.5, 0.1875)
    gain_two = jnp.clip(1.0 + 0.15 * jax.random.normal(seeds[5], (CH_MID,), jnp.float32), 0.25, 1.75)
    shift_two = bell_draw(seeds[6], (CH_MID,), 0.5, 3.0, jnp.float32)
    depth_two = bell_draw(seeds[7], (3, 3, CH_MID), 9 ** -0.5, 2.0)
    gain_three = jnp.clip(1.0 + 0.15 * jax.random.normal(seeds[8], (CH_MID,), jnp.float32), 0.25, 1.75)
    shift_three = bell_draw(seeds[9], (CH_MID,), 0.5, 3.0, jnp.float32)
    point_two = bell_draw(seeds[10], (CH_MID, CH_OUT), CH_MID ** -0.5, 0.15625)
    gain_four = jnp.clip(1.0 + 0.15 * jax.random.normal(seeds[11], (CH_OUT,), jnp.float32), 0.25, 1.75)
    shift_four = bell_draw(seeds[12], (CH_OUT,), 0.5, 3.0, jnp.float32)
    return {"features": features, "depth_one": depth_one, "gain_one": gain_one, "shift_one": shift_one, "point_one": point_one, "gain_two": gain_two, "shift_two": shift_two, "depth_two": depth_two, "gain_three": gain_three, "shift_three": shift_three, "point_two": point_two, "gain_four": gain_four, "shift_four": shift_four}


epsilon = 1e-05

def dilated(values, weight):
    span_rows = values.shape[1]
    span_cols = values.shape[2]
    padded = jnp.pad(values, ((0, 0), (RATE, RATE), (RATE, RATE), (0, 0)))
    summed = jnp.zeros(values.shape, jnp.float32)
    for tap_row in range(3):
        for tap_col in range(3):
            window = padded[:, tap_row * RATE:tap_row * RATE + span_rows, tap_col * RATE:tap_col * RATE + span_cols, :]
            summed = summed + window.astype(jnp.float32) * weight[tap_row, tap_col].astype(jnp.float32)
    return summed

def normalize(values, gain, offset):
    pixels = values.shape[0] * values.shape[1] * values.shape[2]
    average = lax.optimization_barrier(jnp.sum(values, axis=(0, 1, 2))) / pixels
    variance = lax.optimization_barrier(jnp.sum(values * values, axis=(0, 1, 2))) / pixels - average * average
    factor = gain * lax.rsqrt(variance + epsilon)
    return jnp.maximum((values - average) * factor + offset, 0.0).astype(jnp.bfloat16)

def project(values, weight):
    shape = values.shape
    flat = values.reshape(shape[0] * shape[1] * shape[2], shape[3])
    result = jnp.dot(flat, weight, preferred_element_type=jnp.float32)
    return result.reshape(shape[0], shape[1], shape[2], weight.shape[1])

def reference(features, depth_one, gain_one, shift_one, point_one, gain_two, shift_two, depth_two, gain_three, shift_three, point_two, gain_four, shift_four):
    act_one = normalize(dilated(features, depth_one), gain_one, shift_one)
    act_two = normalize(project(act_one, point_one), gain_two, shift_two)
    act_three = normalize(dilated(act_two, depth_two), gain_three, shift_three)
    return normalize(project(act_three, point_two), gain_four, shift_four)
```

```python
import jax
import jax.numpy as jnp
from jax import lax
from jax.sharding import Mesh
from jax.sharding import PartitionSpec as P

RATE = 2
BATCH = ("batch_0", "batch_1")
SPACE = ("space_0", "space_1")


epsilon = 1e-05


def padded_2(cells, sides, width):
    for axis, dim in sides:
        count = lax.axis_size(axis)
        ends = count - 1
        head = lax.slice_in_dim(cells, 0, width, axis=dim)
        tail = lax.slice_in_dim(cells, cells.shape[dim] - width, cells.shape[dim], axis=dim)
        cells = jnp.concatenate(
            [
                lax.ppermute(tail, axis, [(i, (i + 1) % count) for i in range(ends)]),
                cells,
                lax.ppermute(head, axis, [((i + 1) % count, i) for i in range(ends)]),
            ],
            axis=dim,
        )
    return cells


def shared_over(value, axes):
    count = lax.axis_size(axes)
    copies = jnp.broadcast_to(value[None], (count,) + value.shape)
    return jnp.sum(lax.all_to_all(copies, axes, 0, 0), axis=0)


def global_sums(parts):
    value = jnp.stack(parts).reshape(-1, 128)
    value = value + lax.ppermute(value, "space_1", [(0, 1), (1, 0)])
    value = shared_over(value, ("batch_1", "space_0"))
    value = shared_over(value, ("batch_0",))
    return value.reshape(2, -1)


def dilated_padded(padded, weight, span_rows, span_cols):
    summed = jnp.zeros((padded.shape[0], span_rows, span_cols, padded.shape[3]), jnp.float32)
    for tap_row in range(3):
        for tap_col in range(3):
            window = padded[
                :,
                tap_row * RATE : tap_row * RATE + span_rows,
                tap_col * RATE : tap_col * RATE + span_cols,
                :,
            ]
            summed = summed + window.astype(jnp.float32) * weight[tap_row, tap_col].astype(
                jnp.float32
            )
    return summed


def local_sums(values):
    return (jnp.sum(values, axis=(0, 1, 2)), jnp.sum(values * values, axis=(0, 1, 2)))


def scaled(values, totals, pixels, gain, offset):
    average = totals[0] / pixels
    variance = totals[1] / pixels - average * average
    factor = gain * lax.rsqrt(variance + epsilon)
    return jnp.maximum((values - average) * factor + offset, 0.0).astype(jnp.bfloat16)


def project(values, weight):
    shape = values.shape
    flat = values.reshape(shape[0] * shape[1] * shape[2], shape[3])
    result = jnp.dot(flat, weight, preferred_element_type=jnp.float32)
    return result.reshape(shape[0], shape[1], shape[2], weight.shape[1])


def per_device(
    features,
    depth_one,
    gain_one,
    shift_one,
    point_one,
    gain_two,
    shift_two,
    depth_two,
    gain_three,
    shift_three,
    point_two,
    gain_four,
    shift_four,
):
    span_rows = features.shape[1]
    span_cols = features.shape[2]
    n_batch = lax.axis_size(BATCH)
    n_space = lax.axis_size(SPACE)
    all_pixels = features.shape[0] * span_rows * span_cols * n_batch * n_space
    padded = padded_2(features, ((SPACE, 1),), RATE)
    padded = jnp.pad(padded, ((0, 0), (0, 0), (RATE, RATE), (0, 0)))
    first = dilated_padded(padded, depth_one, span_rows, span_cols)
    totals = global_sums(local_sums(first))
    act_one = scaled(first, totals, all_pixels, gain_one, shift_one)
    second = project(act_one, point_one)
    totals = global_sums(local_sums(second))
    act_two = scaled(second, totals, all_pixels, gain_two, shift_two)
    padded = padded_2(act_two, ((SPACE, 1),), RATE)
    padded = jnp.pad(padded, ((0, 0), (0, 0), (RATE, RATE), (0, 0)))
    third = dilated_padded(padded, depth_two, span_rows, span_cols)
    totals = global_sums(local_sums(third))
    act_three = scaled(third, totals, all_pixels, gain_three, shift_three)
    fourth = project(act_three, point_two)
    totals = global_sums(local_sums(fourth))
    return scaled(fourth, totals, all_pixels, gain_four, shift_four)


def solution(mesh):
    finer = Mesh(mesh.devices.reshape(8, 4, 4, 2), ("batch_0", "batch_1", "space_0", "space_1"))
    placed = (
        P(BATCH, SPACE, None, None),
        P(),
        P(),
        P(),
        P(),
        P(),
        P(),
        P(),
        P(),
        P(),
        P(),
        P(),
        P(),
    )
    return jax.shard_map(
        per_device,
        mesh=finer,
        in_specs=placed,
        out_specs=P(BATCH, SPACE, None, None),
        check_vma=False,
    )
```

```python
import functools

import jax
import jax.numpy as jnp
from jax import lax
from jax.experimental import pallas as pl
from jax.experimental.pallas import tpu as pltpu
from jax.sharding import Mesh
from jax.sharding import PartitionSpec as P

RATE = 2
LANES = 128
BATCH = ("batch_0", "batch_1")
SPACE = ("space_0", "space_1")

epsilon = 1e-05

VMEM = pl.BlockSpec(memory_space=pltpu.VMEM)
HBM = pl.BlockSpec(memory_space=pltpu.HBM)


def kernel_call(body, outs, n_in, limit, scratch=(), flops=0, moved=0):
    return pl.pallas_call(
        body,
        out_shape=[pltpu.VMEM(shape, dtype) for shape, dtype in outs],
        in_specs=[VMEM] * n_in,
        out_specs=[VMEM] * len(outs),
        scratch_shapes=list(scratch),
        compiler_params=pltpu.CompilerParams(vmem_limit_bytes=limit),
        cost_estimate=pl.CostEstimate(flops=flops, bytes_accessed=moved, transcendentals=0),
    )


def moved_down(row):
    gap = jnp.zeros((RATE, row.shape[1]), row.dtype)
    return jnp.concatenate([gap, row[: row.shape[0] - RATE]], axis=0)


def moved_up(row):
    gap = jnp.zeros((RATE, row.shape[1]), row.dtype)
    return jnp.concatenate([row[RATE:], gap], axis=0)


def taps_of(filter_ref, lanes):
    return [filter_ref[tap, :, lanes].astype(jnp.float32) for tap in range(3)]


def dilated_row(rows, taps):
    sides = []
    for tap_col in range(3):
        side = None
        for tap_row in range(3):
            term = rows[tap_row] * taps[tap_row][tap_col : tap_col + 1]
            side = term if side is None else side + term
        sides.append(side)
    return sides[1] + moved_down(sides[0]) + moved_up(sides[2])


def summed_rows(value):
    return jnp.sum(value.reshape(value.shape[0] // 8, 8, value.shape[1]), axis=0)


def store_sums(sums_ref, lanes, total, squares):
    sums_ref[0:1, lanes] = jnp.sum(total, axis=0, keepdims=True)
    sums_ref[1:2, lanes] = jnp.sum(squares, axis=0, keepdims=True)


def dilated_rows(row_at, rows, taps, out_ref, lanes):
    total = squares = None
    for place, row in enumerate(rows):
        value = dilated_row([row_at(row - RATE), row_at(row), row_at(row + RATE)], taps)
        out_ref[place, :, lanes] = value
        part, part_squares = summed_rows(value), summed_rows(value * value)
        total = part if total is None else total + part
        squares = part_squares if squares is None else squares + part_squares
    return total, squares


def inner_body(x_hbm, filter_hbm, out_ref, sums_ref, x_ref, filter_ref, arrived, filter_arrived):
    count, _, depth = x_ref.shape
    wide = depth // arrived.shape[0]

    def piece(place):
        lanes = pl.ds(place * wide, wide)
        return pltpu.make_async_copy(
            x_hbm.at[0, :, :, lanes], x_ref.at[:, :, lanes], arrived.at[place]
        )

    taps_copy = pltpu.make_async_copy(filter_hbm, filter_ref, filter_arrived)
    taps_copy.start()
    for place in range(arrived.shape[0]):
        piece(place).start()
    taps_copy.wait()
    for place in range(arrived.shape[0]):
        piece(place).wait()

        @pl.loop(place * wide // LANES, (place + 1) * wide // LANES)
        def _(block):
            lanes = pl.ds(pl.multiple_of(block * LANES, LANES), LANES)
            total, squares = dilated_rows(
                lambda row: x_ref[row, :, lanes].astype(jnp.float32),
                range(RATE, count - RATE),
                taps_of(filter_ref, lanes),
                out_ref,
                lanes,
            )
            store_sums(sums_ref, lanes, total, squares)


def edge_starts(count):
    core = lax.axis_index("space_1")
    return (1 - core) * (count - RATE), core * (count - RATE)


def edge_rows_body(x_hbm, chip_ref, cross_ref, arrived):
    starts = edge_starts(x_hbm.shape[1])
    copies = [
        pltpu.make_async_copy(x_hbm.at[0, pl.ds(start, RATE)], out_ref, arrived.at[place])
        for place, (start, out_ref) in enumerate(zip(starts, (chip_ref, cross_ref)))
    ]
    for copy in copies:
        copy.start()
    for copy in copies:
        copy.wait()


def edge_body(x_ref, chip_ref, cross_ref, filter_ref, inner_ref, out_ref, sums_ref):
    count = x_ref.shape[0]
    core = lax.axis_index("space_1")

    @pl.loop(0, x_ref.shape[2] // LANES)
    def _(block):
        lanes = pl.ds(pl.multiple_of(block * LANES, LANES), LANES)

        @functools.cache
        def row_at(row):
            if row < 0:
                return halo_row(chip_ref, cross_ref, core == 1, row + RATE, lanes)
            if row >= count:
                return halo_row(chip_ref, cross_ref, core == 0, row - count, lanes)
            return x_ref[row, :, lanes].astype(jnp.float32)

        rows = (*range(RATE), *range(count - RATE, count))
        total, squares = dilated_rows(row_at, rows, taps_of(filter_ref, lanes), out_ref, lanes)
        store_sums(sums_ref, lanes, total, squares)
        sums_ref[:, lanes] = sums_ref[:, lanes] + inner_ref[:, lanes]


def store_terms(terms_ref, parts_ref, gain_ref, shift_ref, pixels):
    for block in range(gain_ref.shape[0]):
        lanes = slice(block * LANES, (block + 1) * LANES)
        sums = jnp.sum(parts_ref[:, :, lanes], axis=0)
        average = sums[0:1] / pixels
        variance = sums[1:2] / pixels - average * average
        factor = gain_ref[block : block + 1] * lax.rsqrt(variance + epsilon)
        terms_ref[0:1, lanes] = factor
        terms_ref[1:2, lanes] = shift_ref[block : block + 1] - average * factor


def halo_row(chip_ref, cross_ref, chip_holds, row, lanes):
    return jnp.where(chip_holds, chip_ref[row, :, lanes], cross_ref[row, :, lanes]).astype(jnp.float32)


def third_body(
    pixels, u_ref, chip_ref, cross_ref, parts_ref, gain_ref, shift_ref, filter_ref,
    out_ref, sums_ref, terms_ref,
):
    count = u_ref.shape[0]
    store_terms(terms_ref, parts_ref, gain_ref, shift_ref, pixels)

    @pl.loop(0, u_ref.shape[2] // LANES)
    def _(block):
        lanes = pl.ds(pl.multiple_of(block * LANES, LANES), LANES)
        taps = taps_of(filter_ref, lanes)
        factor = terms_ref[0:1, lanes]
        offset = terms_ref[1:2, lanes]
        core = lax.axis_index("space_1")
        strip = lax.axis_index(SPACE)
        above = (strip > 0).astype(jnp.float32)
        below = (strip < lax.axis_size(SPACE) - 1).astype(jnp.float32)

        @functools.cache
        def row_at(row):
            if row < 0:
                value = halo_row(chip_ref, cross_ref, core == 1, row + RATE, lanes)
                value = value * (factor * above) + offset * above
            elif row >= count:
                value = halo_row(chip_ref, cross_ref, core == 0, row - count, lanes)
                value = value * (factor * below) + offset * below
            else:
                value = u_ref[row, :, lanes] * factor + offset
            return jnp.maximum(value, 0.0).astype(jnp.bfloat16).astype(jnp.float32)

        total, squares = dilated_rows(row_at, range(count), taps, out_ref, lanes)
        store_sums(sums_ref, lanes, total, squares)


def project_body(pixels, places, n_parts, n_edges, *refs):
    part_refs = refs[:n_parts]
    parts_ref, gain_ref, shift_ref, weight_hbm, out_ref, sums_ref = refs[n_parts : n_parts + 6]
    edge_refs = refs[n_parts + 6 : n_parts + 6 + n_edges]
    terms_ref, act_ref, weight_ref, arrived = refs[n_parts + 6 + n_edges :]
    count, cols, width = out_ref.shape
    depth = act_ref.shape[1]
    wide = width // arrived.shape[0]

    def piece(block, lanes):
        return pltpu.make_async_copy(
            weight_hbm.at[:, lanes], weight_ref.at[:, lanes], arrived.at[block]
        )

    for block in range(arrived.shape[0]):
        piece(block, pl.ds(block * wide, wide)).start()
    store_terms(terms_ref, parts_ref, gain_ref, shift_ref, pixels)
    pair = 2
    for u_ref, first_row in zip(part_refs, places):

        @pl.loop(0, u_ref.shape[0] // pair)
        def _(step):
            factor = terms_ref[0:1]
            offset = terms_ref[1:2]
            value = u_ref[pl.ds(step * pair, pair)].reshape(pair * cols, depth)
            row = first_row + step * pair
            if len(places) > 1 and first_row == 0:
                row = step * (count - pair)
            act_ref[pl.ds(pl.multiple_of(row * cols, pair * cols), pair * cols)] = jnp.maximum(
                value * factor + offset, 0.0
            ).astype(jnp.bfloat16)

    @pl.loop(0, arrived.shape[0])
    def _(block):
        lanes = pl.ds(pl.multiple_of(block * wide, wide), wide)
        piece(block, lanes).wait()
        result = jnp.dot(act_ref[...], weight_ref[:, lanes], preferred_element_type=jnp.float32)
        store_sums(sums_ref, lanes, summed_rows(result), summed_rows(result * result))
        result = result.reshape(count, cols, wide)
        out_ref[:, :, lanes] = result
        for edge_ref, start in zip(edge_refs, edge_starts(count)):
            edge_ref[:, :, lanes] = out_ref[pl.ds(start, RATE), :, lanes]


def last_body(pixels, u_ref, parts_ref, gain_ref, shift_ref, out_ref, terms_ref):
    @pl.when(pl.program_id(0) == 0)
    def _():
        store_terms(terms_ref, parts_ref, gain_ref, shift_ref, pixels)

    rows = out_ref.shape[1]
    value = u_ref[pl.ds(pl.program_id(0) * rows, rows)]
    out_ref[0] = jnp.maximum(value * terms_ref[0:1] + terms_ref[1:2], 0.0).astype(jnp.bfloat16)


def dilated_inner(x, weight):
    rows, cols, depth = x.shape[1:]
    inner = rows - 2 * RATE
    return pl.pallas_call(
        inner_body,
        out_shape=[
            pltpu.VMEM((inner, cols, depth), jnp.float32),
            pltpu.VMEM((2, depth), jnp.float32),
            pltpu.VMEM((rows, cols, depth), x.dtype),
            pltpu.VMEM(weight.shape, weight.dtype),
        ],
        in_specs=[HBM] * 2,
        out_specs=[VMEM] * 4,
        scratch_shapes=[pltpu.SemaphoreType.DMA((4,)), pltpu.SemaphoreType.DMA],
        compiler_params=pltpu.CompilerParams(vmem_limit_bytes=12 << 20),
        cost_estimate=pl.CostEstimate(
            flops=20 * inner * cols * depth, bytes_accessed=6 * rows * cols * depth, transcendentals=0
        ),
    )(x, weight)


def kept_in_hbm(array):
    return pltpu.with_memory_space_constraint(array, pltpu.HBM)


def edge_rows(x):
    edge = (RATE,) + x.shape[2:]
    return pl.pallas_call(
        edge_rows_body,
        out_shape=[pltpu.VMEM(edge, x.dtype)] * 2,
        in_specs=[HBM],
        out_specs=[VMEM] * 2,
        scratch_shapes=[pltpu.SemaphoreType.DMA((2,))],
        compiler_params=pltpu.CompilerParams(vmem_limit_bytes=4 << 20),
    )(x)


def dilated_edges(x, chip, cross, weight, inner_sums):
    cols, depth = x.shape[1:]
    return kernel_call(
        edge_body,
        [((2 * RATE, cols, depth), jnp.float32), ((2, depth), jnp.float32)],
        5,
        12 << 20,
        flops=40 * RATE * cols * depth,
        moved=20 * RATE * cols * depth,
    )(x, chip, cross, weight, inner_sums)


def project(pixels, pieces, places, parts, gain, shift, weight, edges):
    rows = sum(piece.shape[0] for piece in pieces)
    cols, depth = pieces[0].shape[1:]
    width = weight.shape[1]
    outs = [((rows, cols, width), jnp.float32), ((2, width), jnp.float32)]
    outs += [((RATE, cols, width), jnp.float32)] * edges
    return pl.pallas_call(
        functools.partial(project_body, pixels, places, len(pieces), edges),
        out_shape=[pltpu.VMEM(shape, dtype) for shape, dtype in outs],
        in_specs=[VMEM] * (len(pieces) + 3) + [HBM],
        out_specs=[VMEM] * len(outs),
        scratch_shapes=[
            pltpu.VMEM((2, depth), jnp.float32),
            pltpu.VMEM((rows * cols, depth), jnp.bfloat16),
            pltpu.VMEM((depth, width), jnp.bfloat16),
            pltpu.SemaphoreType.DMA((width // 256,)),
        ],
        compiler_params=pltpu.CompilerParams(vmem_limit_bytes=24 << 20),
        cost_estimate=pl.CostEstimate(
            flops=2 * rows * cols * depth * width,
            bytes_accessed=4 * rows * cols * (depth + width) + 2 * depth * width,
            transcendentals=0,
        ),
    )(*pieces, parts, gain, shift, weight)


def dilated_second(pixels, u, chip, cross, parts, gain, shift, weight):
    rows, cols, depth = u.shape
    return kernel_call(
        functools.partial(third_body, pixels),
        [((rows, cols, depth), jnp.float32), ((2, depth), jnp.float32)],
        7,
        16 << 20,
        scratch=[pltpu.VMEM((2, depth), jnp.float32)],
        flops=26 * rows * cols * depth,
        moved=8 * rows * cols * depth,
    )(u, chip, cross, parts, gain, shift, weight)


def last_norm(pixels, u, parts, gain, shift):
    rows, cols, depth = u.shape
    return pl.pallas_call(
        functools.partial(last_body, pixels),
        grid=(rows // 3,),
        out_shape=jax.ShapeDtypeStruct((1, rows, cols, depth), jnp.bfloat16),
        in_specs=[VMEM] * 4,
        out_specs=pl.BlockSpec((1, 3, cols, depth), lambda row: (0, row, 0, 0)),
        scratch_shapes=[pltpu.VMEM((2, depth), jnp.float32)],
        compiler_params=pltpu.CompilerParams(vmem_limit_bytes=20 << 20),
        cost_estimate=pl.CostEstimate(
            flops=3 * rows * cols * depth, bytes_accessed=6 * rows * cols * depth, transcendentals=0
        ),
    )(u, parts, gain, shift)


def pair_body(own_ref, other_ref, out_ref):
    out_ref[...] = jnp.broadcast_to((own_ref[...] + other_ref[...])[None], out_ref.shape)


def group_body(parts_ref, out_ref):
    out_ref[...] = jnp.broadcast_to(jnp.sum(parts_ref[...], axis=0)[None], out_ref.shape)


def gathered_sums(value):
    plane, line = ("batch_1", "space_0"), ("batch_0",)
    other = lax.ppermute(value, "space_1", [(0, 1), (1, 0)])
    shape = (lax.axis_size(plane),) + value.shape
    (copies,) = kernel_call(pair_body, [(shape, jnp.float32)], 2, 2 << 20)(value, other)
    parts = lax.all_to_all(copies, plane, 0, 0)
    shape = (lax.axis_size(line),) + value.shape
    (copies,) = kernel_call(group_body, [(shape, jnp.float32)], 1, 2 << 20)(parts)
    return lax.all_to_all(copies, line, 0, 0)


def from_neighbours(chip, cross):
    ends = [pair for i in range(1, lax.axis_size(SPACE) - 1, 2) for pair in ((i, i + 1), (i + 1, i))]
    chip = lax.ppermute(chip, "space_1", [(0, 1), (1, 0)])
    return chip, lax.ppermute(cross, SPACE, ends)


def per_device(
    features,
    depth_one,
    gain_one,
    shift_one,
    point_one,
    gain_two,
    shift_two,
    depth_two,
    gain_three,
    shift_three,
    point_two,
    gain_four,
    shift_four,
):
    rows, cols = features.shape[1:3]
    pixels = rows * cols * lax.axis_size(BATCH) * lax.axis_size(SPACE)
    names = (gain_one, shift_one, gain_two, shift_two, gain_three, shift_three, gain_four, shift_four)
    terms = [term.reshape(-1, LANES) for term in names]
    features, depth_one = kept_in_hbm(features), kept_in_hbm(depth_one)
    halo = from_neighbours(*edge_rows(features))
    inner, inner_sums, x, taps = dilated_inner(features, depth_one)
    edges, sums = dilated_edges(x, *halo, taps, inner_sums)
    parts = gathered_sums(sums)
    second, sums, chip, cross = project(
        pixels, (edges, inner), (0, RATE), parts, *terms[0:2], kept_in_hbm(point_one), 2
    )
    halo = from_neighbours(chip, cross)
    parts = gathered_sums(sums)
    third, sums = dilated_second(pixels, second, *halo, parts, *terms[2:4], depth_two)
    parts = gathered_sums(sums)
    fourth, sums = project(pixels, (third,), (0,), parts, *terms[4:6], kept_in_hbm(point_two), 0)
    parts = gathered_sums(sums)
    return last_norm(pixels, fourth, parts, *terms[6:8])


def solution(mesh):
    finer = Mesh(mesh.devices.reshape(8, 4, 4, 2), ("batch_0", "batch_1", "space_0", "space_1"))
    placed = (P(BATCH, SPACE, None, None),) + (P(),) * 12
    return jax.shard_map(
        per_device,
        mesh=finer,
        in_specs=placed,
        out_specs=P(BATCH, SPACE, None, None),
        check_vma=False,
    )
```

```python
import functools

import jax
import jax.numpy as jnp
from jax import lax
from jax.experimental import pallas as pl
from jax.experimental.pallas import tpu as pltpu
from jax.sharding import Mesh
from jax.sharding import PartitionSpec as P

RATE = 2
LANES = 128
OFFSET_ROWS = 8
BATCH = ("batch_0", "batch_1")
SPACE = ("space_0", "space_1")

epsilon = 1e-05

VMEM = pl.BlockSpec(memory_space=pltpu.VMEM)
HBM = pl.BlockSpec(memory_space=pltpu.HBM)


def kernel_call(body, outs, n_in, limit, scratch=(), flops=0, moved=0):
    return pl.pallas_call(
        body,
        out_shape=[pltpu.VMEM(shape, dtype) for shape, dtype in outs],
        in_specs=[VMEM] * n_in,
        out_specs=[VMEM] * len(outs),
        scratch_shapes=list(scratch),
        compiler_params=pltpu.CompilerParams(vmem_limit_bytes=limit),
        cost_estimate=pl.CostEstimate(flops=flops, bytes_accessed=moved, transcendentals=0),
    )


def moved_down(row):
    gap = jnp.zeros((RATE, row.shape[1]), row.dtype)
    return jnp.concatenate([gap, row[: row.shape[0] - RATE]], axis=0)


def moved_up(row):
    gap = jnp.zeros((RATE, row.shape[1]), row.dtype)
    return jnp.concatenate([row[RATE:], gap], axis=0)


def taps_of(filter_ref, lanes):
    return [filter_ref[tap, :, lanes].astype(jnp.float32) for tap in range(3)]


def dilated_row(rows, taps):
    sides = []
    for tap_col in range(3):
        side = None
        for tap_row in range(3):
            term = rows[tap_row] * taps[tap_row][tap_col : tap_col + 1]
            side = term if side is None else side + term
        sides.append(side)
    return sides[1] + moved_down(sides[0]) + moved_up(sides[2])


def summed_rows(value):
    return jnp.sum(value.reshape(value.shape[0] // 8, 8, value.shape[1]), axis=0)


def store_sums(sums_ref, lanes, total, squares):
    sums_ref[0:1, lanes] = jnp.sum(total, axis=0, keepdims=True)
    sums_ref[1:2, lanes] = jnp.sum(squares, axis=0, keepdims=True)


def dilated_rows(row_at, rows, taps, out_ref, lanes):
    total = squares = None
    for place, row in sorted(enumerate(rows), key=lambda pair: (pair[1] % 2, pair[1])):
        value = dilated_row([row_at(row - RATE), row_at(row), row_at(row + RATE)], taps)
        out_ref[place, :, lanes] = value
        part, part_squares = summed_rows(value), summed_rows(value * value)
        total = part if total is None else total + part
        squares = part_squares if squares is None else squares + part_squares
    return total, squares


def inner_body(
    x_hbm, filter_hbm, weight_hbm, out_ref, sums_ref, x_ref, filter_ref, weight_ref, arrived,
    filter_arrived, weight_arrived,
):
    count, _, depth = x_ref.shape
    wide = depth // arrived.shape[0]

    def piece(place):
        lanes = pl.ds(place * wide, wide)
        return pltpu.make_async_copy(
            x_hbm.at[0, :, :, lanes], x_ref.at[:, :, lanes], arrived.at[place]
        )

    taps_copy = pltpu.make_async_copy(filter_hbm, filter_ref, filter_arrived)
    taps_copy.start()
    for place in range(arrived.shape[0]):
        piece(place).start()
    weight_copy = pltpu.make_async_copy(weight_hbm, weight_ref, weight_arrived)
    weight_copy.start()
    taps_copy.wait()
    for place in range(arrived.shape[0]):
        piece(place).wait()

        @pl.loop(place * wide // LANES, (place + 1) * wide // LANES)
        def _(block):
            lanes = pl.ds(pl.multiple_of(block * LANES, LANES), LANES)
            total, squares = dilated_rows(
                functools.cache(lambda row: x_ref[row, :, lanes].astype(jnp.float32)),
                range(RATE, count - RATE),
                taps_of(filter_ref, lanes),
                out_ref,
                lanes,
            )
            store_sums(sums_ref, lanes, total, squares)

    weight_copy.wait()


def edge_starts(count):
    core = lax.axis_index("space_1")
    return (1 - core) * (count - RATE), core * (count - RATE)


def edge_rows_body(x_hbm, chip_ref, cross_ref, arrived):
    starts = edge_starts(x_hbm.shape[1])
    copies = [
        pltpu.make_async_copy(x_hbm.at[0, pl.ds(start, RATE)], out_ref, arrived.at[place])
        for place, (start, out_ref) in enumerate(zip(starts, (chip_ref, cross_ref)))
    ]
    for copy in copies:
        copy.start()
    for copy in copies:
        copy.wait()


def edge_body(x_ref, chip_ref, cross_ref, filter_ref, inner_ref, out_ref, sums_ref):
    count = x_ref.shape[0]
    core = lax.axis_index("space_1")

    @pl.loop(0, x_ref.shape[2] // LANES)
    def _(block):
        lanes = pl.ds(pl.multiple_of(block * LANES, LANES), LANES)

        @functools.cache
        def row_at(row):
            if row < 0:
                return halo_row(chip_ref, cross_ref, core == 1, row + RATE, lanes)
            if row >= count:
                return halo_row(chip_ref, cross_ref, core == 0, row - count, lanes)
            return x_ref[row, :, lanes].astype(jnp.float32)

        rows = (*range(RATE), *range(count - RATE, count))
        total, squares = dilated_rows(row_at, rows, taps_of(filter_ref, lanes), out_ref, lanes)
        store_sums(sums_ref, lanes, total, squares)
        sums_ref[:, lanes] = sums_ref[:, lanes] + inner_ref[:, lanes]


def store_terms(terms_ref, parts_ref, gain_ref, shift_ref, pixels):
    for block in range(gain_ref.shape[0]):
        lanes = slice(block * LANES, (block + 1) * LANES)
        sums = jnp.sum(parts_ref[:, :, lanes], axis=0)
        average = sums[0:1] / pixels
        variance = sums[1:2] / pixels - average * average
        factor = gain_ref[block : block + 1] * lax.rsqrt(variance + epsilon)
        terms_ref[0:1, lanes] = factor
        terms_ref[1:2, lanes] = shift_ref[block : block + 1] - average * factor


def halo_row(chip_ref, cross_ref, chip_holds, row, lanes):
    return jnp.where(chip_holds, chip_ref[row, :, lanes], cross_ref[row, :, lanes]).astype(jnp.float32)


def less_offset(row, offset):
    last = jnp.broadcast_to(offset, (OFFSET_ROWS, offset.shape[1]))
    return jnp.concatenate([row - offset, last], axis=0).astype(jnp.bfloat16)


def restored_row(chip_ref, cross_ref, chip_holds, row, lanes):
    value = halo_row(chip_ref, cross_ref, chip_holds, row, lanes)
    cols = value.shape[0] - OFFSET_ROWS
    return value[:cols] + value[cols : cols + 1]


def third_body(
    pixels, u_ref, chip_ref, cross_ref, parts_ref, gain_ref, shift_ref, filter_ref,
    weight_hbm, out_ref, sums_ref, weight_ref, terms_ref, arrived,
):
    count = u_ref.shape[0]
    weight_copy = pltpu.make_async_copy(weight_hbm, weight_ref, arrived)
    weight_copy.start()
    store_terms(terms_ref, parts_ref, gain_ref, shift_ref, pixels)

    @pl.loop(0, u_ref.shape[2] // LANES)
    def _(block):
        lanes = pl.ds(pl.multiple_of(block * LANES, LANES), LANES)
        taps = taps_of(filter_ref, lanes)
        factor = terms_ref[0:1, lanes]
        offset = terms_ref[1:2, lanes]
        core = lax.axis_index("space_1")
        strip = lax.axis_index(SPACE)
        above = (strip > 0).astype(jnp.float32)
        below = (strip < lax.axis_size(SPACE) - 1).astype(jnp.float32)

        @functools.cache
        def row_at(row):
            if row < 0:
                value = restored_row(chip_ref, cross_ref, core == 1, row + RATE, lanes)
                value = value * (factor * above) + offset * above
            elif row >= count:
                value = restored_row(chip_ref, cross_ref, core == 0, row - count, lanes)
                value = value * (factor * below) + offset * below
            else:
                value = u_ref[row, :, lanes] * factor + offset
            return jnp.maximum(value, 0.0)

        total, squares = dilated_rows(row_at, range(count), taps, out_ref, lanes)
        store_sums(sums_ref, lanes, total, squares)

    weight_copy.wait()


def project_body(pixels, places, n_parts, n_edges, *refs):
    part_refs = refs[:n_parts]
    parts_ref, gain_ref, shift_ref, weight_ref, out_ref, sums_ref = refs[n_parts : n_parts + 6]
    edge_refs = refs[n_parts + 6 : n_parts + 6 + n_edges]
    terms_ref, act_ref = refs[n_parts + 6 + n_edges :]
    count, cols, width = out_ref.shape
    depth = act_ref.shape[1]
    wide = 512
    store_terms(terms_ref, parts_ref, gain_ref, shift_ref, pixels)
    pair = 2
    for u_ref, first_row in zip(part_refs, places):

        @pl.loop(0, u_ref.shape[0] // pair)
        def _(step):
            factor = terms_ref[0:1]
            offset = terms_ref[1:2]
            value = u_ref[pl.ds(step * pair, pair)].reshape(pair * cols, depth)
            row = first_row + step * pair
            if len(places) > 1 and first_row == 0:
                row = step * (count - pair)
            act_ref[pl.ds(pl.multiple_of(row * cols, pair * cols), pair * cols)] = jnp.maximum(
                value * factor + offset, 0.0
            ).astype(jnp.bfloat16)

    @pl.loop(0, width // wide)
    def _(block):
        lanes = pl.ds(pl.multiple_of(block * wide, wide), wide)
        result = jnp.dot(act_ref[...], weight_ref[:, lanes], preferred_element_type=jnp.float32)
        store_sums(sums_ref, lanes, summed_rows(result), summed_rows(result * result))
        out_ref[:, :, lanes] = result.reshape(count, cols, wide)
        offset = (sums_ref[0:1, lanes] / (count * cols)).astype(jnp.bfloat16).astype(jnp.float32)
        for edge_ref, start in zip(edge_refs, edge_starts(count)):
            for row in range(RATE):
                edge_ref[row, :, lanes] = less_offset(out_ref[start + row, :, lanes], offset)


def last_body(pixels, u_ref, parts_ref, gain_ref, shift_ref, out_ref, terms_ref):
    @pl.when(pl.program_id(0) == 0)
    def _():
        store_terms(terms_ref, parts_ref, gain_ref, shift_ref, pixels)

    rows = out_ref.shape[1]
    value = u_ref[pl.ds(pl.program_id(0) * rows, rows)]
    out_ref[0] = jnp.maximum(value * terms_ref[0:1] + terms_ref[1:2], 0.0).astype(jnp.bfloat16)


def dilated_inner(x, taps, weight):
    rows, cols, depth = x.shape[1:]
    inner = rows - 2 * RATE
    return pl.pallas_call(
        inner_body,
        out_shape=[
            pltpu.VMEM((inner, cols, depth), jnp.float32),
            pltpu.VMEM((2, depth), jnp.float32),
            pltpu.VMEM((rows, cols, depth), x.dtype),
            pltpu.VMEM(taps.shape, taps.dtype),
            pltpu.VMEM(weight.shape, weight.dtype),
        ],
        in_specs=[HBM] * 3,
        out_specs=[VMEM] * 5,
        scratch_shapes=[pltpu.SemaphoreType.DMA((4,))] + [pltpu.SemaphoreType.DMA] * 2,
        compiler_params=pltpu.CompilerParams(vmem_limit_bytes=12 << 20),
        cost_estimate=pl.CostEstimate(
            flops=20 * inner * cols * depth, bytes_accessed=6 * rows * cols * depth, transcendentals=0
        ),
    )(x, taps, weight)


def kept_in_hbm(array):
    return pltpu.with_memory_space_constraint(array, pltpu.HBM)


def edge_rows(x):
    edge = (RATE,) + x.shape[2:]
    return pl.pallas_call(
        edge_rows_body,
        out_shape=[pltpu.VMEM(edge, x.dtype)] * 2,
        in_specs=[HBM],
        out_specs=[VMEM] * 2,
        scratch_shapes=[pltpu.SemaphoreType.DMA((2,))],
        compiler_params=pltpu.CompilerParams(vmem_limit_bytes=4 << 20),
    )(x)


def dilated_edges(x, chip, cross, weight, inner_sums):
    cols, depth = x.shape[1:]
    return kernel_call(
        edge_body,
        [((2 * RATE, cols, depth), jnp.float32), ((2, depth), jnp.float32)],
        5,
        12 << 20,
        flops=40 * RATE * cols * depth,
        moved=20 * RATE * cols * depth,
    )(x, chip, cross, weight, inner_sums)


def project(pixels, pieces, places, parts, gain, shift, weight, edges):
    rows = sum(piece.shape[0] for piece in pieces)
    cols, depth = pieces[0].shape[1:]
    width = weight.shape[1]
    outs = [((rows, cols, width), jnp.float32), ((2, width), jnp.float32)]
    outs += [((RATE, cols + OFFSET_ROWS, width), jnp.bfloat16)] * edges
    return pl.pallas_call(
        functools.partial(project_body, pixels, places, len(pieces), edges),
        out_shape=[pltpu.VMEM(shape, dtype) for shape, dtype in outs],
        in_specs=[VMEM] * (len(pieces) + 4),
        out_specs=[VMEM] * len(outs),
        scratch_shapes=[
            pltpu.VMEM((2, depth), jnp.float32),
            pltpu.VMEM((rows * cols, depth), jnp.bfloat16),
        ],
        compiler_params=pltpu.CompilerParams(vmem_limit_bytes=24 << 20),
        cost_estimate=pl.CostEstimate(
            flops=2 * rows * cols * depth * width,
            bytes_accessed=4 * rows * cols * (depth + width) + 2 * depth * width,
            transcendentals=0,
        ),
    )(*pieces, parts, gain, shift, weight)


def dilated_second(pixels, u, chip, cross, parts, gain, shift, taps, weight):
    rows, cols, depth = u.shape
    return pl.pallas_call(
        functools.partial(third_body, pixels),
        out_shape=[
            pltpu.VMEM((rows, cols, depth), jnp.float32),
            pltpu.VMEM((2, depth), jnp.float32),
            pltpu.VMEM(weight.shape, weight.dtype),
        ],
        in_specs=[VMEM] * 7 + [HBM],
        out_specs=[VMEM] * 3,
        scratch_shapes=[pltpu.VMEM((2, depth), jnp.float32), pltpu.SemaphoreType.DMA],
        compiler_params=pltpu.CompilerParams(vmem_limit_bytes=16 << 20),
        cost_estimate=pl.CostEstimate(
            flops=26 * rows * cols * depth, bytes_accessed=8 * rows * cols * depth, transcendentals=0
        ),
    )(u, chip, cross, parts, gain, shift, taps, weight)


def last_norm(pixels, u, parts, gain, shift):
    rows, cols, depth = u.shape
    return pl.pallas_call(
        functools.partial(last_body, pixels),
        grid=(rows // 3,),
        out_shape=jax.ShapeDtypeStruct((1, rows, cols, depth), jnp.bfloat16),
        in_specs=[VMEM] * 4,
        out_specs=pl.BlockSpec((1, 3, cols, depth), lambda row: (0, row, 0, 0)),
        scratch_shapes=[pltpu.VMEM((2, depth), jnp.float32)],
        compiler_params=pltpu.CompilerParams(vmem_limit_bytes=20 << 20),
        cost_estimate=pl.CostEstimate(
            flops=3 * rows * cols * depth, bytes_accessed=6 * rows * cols * depth, transcendentals=0
        ),
    )(u, parts, gain, shift)


def pair_body(own_ref, other_ref, out_ref):
    out_ref[...] = jnp.broadcast_to((own_ref[...] + other_ref[...])[None], out_ref.shape)


def group_body(parts_ref, out_ref):
    out_ref[...] = jnp.broadcast_to(jnp.sum(parts_ref[...], axis=0)[None], out_ref.shape)


def gathered_sums(value):
    plane, line = ("batch_1", "space_0"), ("batch_0",)
    other = lax.ppermute(value, "space_1", [(0, 1), (1, 0)])
    shape = (lax.axis_size(plane),) + value.shape
    (copies,) = kernel_call(pair_body, [(shape, jnp.float32)], 2, 2 << 20)(value, other)
    parts = lax.all_to_all(copies, plane, 0, 0)
    shape = (lax.axis_size(line),) + value.shape
    (copies,) = kernel_call(group_body, [(shape, jnp.float32)], 1, 2 << 20)(parts)
    return lax.all_to_all(copies, line, 0, 0)


def from_neighbours(chip, cross):
    ends = [pair for i in range(1, lax.axis_size(SPACE) - 1, 2) for pair in ((i, i + 1), (i + 1, i))]
    chip = lax.ppermute(chip, "space_1", [(0, 1), (1, 0)])
    return chip, lax.ppermute(cross, SPACE, ends)


def per_device(
    features,
    depth_one,
    gain_one,
    shift_one,
    point_one,
    gain_two,
    shift_two,
    depth_two,
    gain_three,
    shift_three,
    point_two,
    gain_four,
    shift_four,
):
    rows, cols = features.shape[1:3]
    pixels = rows * cols * lax.axis_size(BATCH) * lax.axis_size(SPACE)
    names = (gain_one, shift_one, gain_two, shift_two, gain_three, shift_three, gain_four, shift_four)
    terms = [term.reshape(-1, LANES) for term in names]
    features, depth_one = kept_in_hbm(features), kept_in_hbm(depth_one)
    halo = from_neighbours(*edge_rows(features))
    inner, inner_sums, x, taps, weight = dilated_inner(features, depth_one, kept_in_hbm(point_one))
    edges, sums = dilated_edges(x, *halo, taps, inner_sums)
    parts = gathered_sums(sums)
    second, sums, chip, cross = project(
        pixels, (edges, inner), (0, RATE), parts, *terms[0:2], weight, 2
    )
    halo = from_neighbours(chip, cross)
    parts = gathered_sums(sums)
    third, sums, weight = dilated_second(
        pixels, second, *halo, parts, *terms[2:4], depth_two, kept_in_hbm(point_two)
    )
    parts = gathered_sums(sums)
    fourth, sums = project(pixels, (third,), (0,), parts, *terms[4:6], weight, 0)
    parts = gathered_sums(sums)
    return last_norm(pixels, fourth, parts, *terms[6:8])


def solution(mesh):
    finer = Mesh(mesh.devices.reshape(8, 4, 4, 2), ("batch_0", "batch_1", "space_0", "space_1"))
    placed = (P(BATCH, SPACE, None, None),) + (P(),) * 12
    return jax.shard_map(
        per_device,
        mesh=finer,
        in_specs=placed,
        out_specs=P(BATCH, SPACE, None, None),
        check_vma=False,
    )
```

```python
import functools

import jax
import jax.numpy as jnp
from jax import lax
from jax.experimental import pallas as pl
from jax.experimental.pallas import tpu as pltpu
from jax.sharding import Mesh
from jax.sharding import PartitionSpec as P

RATE = 2
LANES = 128
BATCH = ("batch_0", "batch_1")
SPACE = ("space_0", "space_1")

epsilon = 1e-05

VMEM = pl.BlockSpec(memory_space=pltpu.VMEM)
HBM = pl.BlockSpec(memory_space=pltpu.HBM)


def kernel_call(body, outs, n_in, limit, scratch=(), flops=0, moved=0):
    return pl.pallas_call(
        body,
        out_shape=[pltpu.VMEM(shape, dtype) for shape, dtype in outs],
        in_specs=[VMEM] * n_in,
        out_specs=[VMEM] * len(outs),
        scratch_shapes=list(scratch),
        compiler_params=pltpu.CompilerParams(vmem_limit_bytes=limit),
        cost_estimate=pl.CostEstimate(flops=flops, bytes_accessed=moved, transcendentals=0),
    )


def moved_down(row):
    gap = jnp.zeros((RATE, row.shape[1]), row.dtype)
    return jnp.concatenate([gap, row[: row.shape[0] - RATE]], axis=0)


def moved_up(row):
    gap = jnp.zeros((RATE, row.shape[1]), row.dtype)
    return jnp.concatenate([row[RATE:], gap], axis=0)


def taps_of(filter_ref, lanes):
    return [filter_ref[tap, :, lanes].astype(jnp.float32) for tap in range(3)]


def dilated_row(rows, taps):
    sides = []
    for tap_col in range(3):
        side = None
        for tap_row in range(3):
            term = rows[tap_row] * taps[tap_row][tap_col : tap_col + 1]
            side = term if side is None else side + term
        sides.append(side)
    return sides[1] + moved_down(sides[0]) + moved_up(sides[2])


def summed_rows(value):
    return jnp.sum(value.reshape(value.shape[0] // 8, 8, value.shape[1]), axis=0)


def store_sums(sums_ref, lanes, total, squares):
    sums_ref[0:1, lanes] = jnp.sum(total, axis=0, keepdims=True)
    sums_ref[1:2, lanes] = jnp.sum(squares, axis=0, keepdims=True)


def dilated_rows(row_at, rows, taps, out_ref, lanes):
    total = squares = None
    for place, row in sorted(enumerate(rows), key=lambda pair: (pair[1] % 2, pair[1])):
        value = dilated_row([row_at(row - RATE), row_at(row), row_at(row + RATE)], taps)
        out_ref[place, :, lanes] = value
        part, part_squares = summed_rows(value), summed_rows(value * value)
        total = part if total is None else total + part
        squares = part_squares if squares is None else squares + part_squares
    return total, squares


def inner_body(x_ref, filter_ref, weight_hbm, out_ref, sums_ref, weight_ref, arrived):
    count = x_ref.shape[0]
    weight_copy = pltpu.make_async_copy(weight_hbm, weight_ref, arrived)
    weight_copy.start()

    @pl.loop(0, x_ref.shape[2] // LANES)
    def _(block):
        lanes = pl.ds(pl.multiple_of(block * LANES, LANES), LANES)
        total, squares = dilated_rows(
            functools.cache(lambda row: x_ref[row, :, lanes].astype(jnp.float32)),
            range(RATE, count - RATE),
            taps_of(filter_ref, lanes),
            out_ref,
            lanes,
        )
        store_sums(sums_ref, lanes, total, squares)

    weight_copy.wait()


def edge_starts(count):
    core = lax.axis_index("space_1")
    return (
        (1 - core) * (count - 2 * RATE),
        core * (count - RATE),
        RATE + core * (count - 3 * RATE),
    )


def load_body(x_hbm, filter_hbm, chip_ref, near_ref, far_ref, x_ref, filter_ref, arrived):
    starts = edge_starts(x_hbm.shape[1])
    copies = [
        pltpu.make_async_copy(
            x_hbm.at[0, pl.ds(start, out_ref.shape[0])], out_ref, arrived.at[place]
        )
        for place, (start, out_ref) in enumerate(zip(starts, (chip_ref, near_ref, far_ref)))
    ]
    copies.append(pltpu.make_async_copy(x_hbm.at[0], x_ref, arrived.at[3]))
    copies.append(pltpu.make_async_copy(filter_hbm, filter_ref, arrived.at[4]))
    for copy in copies:
        copy.start()
    for copy in copies:
        copy.wait()


def halo_row(chip_ref, near_ref, far_ref, row, count, lanes):
    core = lax.axis_index("space_1")
    if row < 0:
        chip_holds, chip_row = core == 1, row + 2 * RATE
        cross_ref, cross_row = (near_ref, row + RATE) if row >= -RATE else (far_ref, row + 2 * RATE)
    else:
        chip_holds, chip_row = core == 0, row - count
        cross_ref, cross_row = (
            (near_ref, row - count) if row < count + RATE else (far_ref, row - count - RATE)
        )
    value = jnp.where(chip_holds, chip_ref[chip_row, :, lanes], cross_ref[cross_row, :, lanes])
    return value.astype(jnp.float32)


def edge_body(x_ref, chip_ref, near_ref, filter_ref, inner_ref, out_ref, sums_ref):
    count = x_ref.shape[0]

    @pl.loop(0, x_ref.shape[2] // LANES)
    def _(block):
        lanes = pl.ds(pl.multiple_of(block * LANES, LANES), LANES)

        @functools.cache
        def row_at(row):
            if 0 <= row < count:
                return x_ref[row, :, lanes].astype(jnp.float32)
            return halo_row(chip_ref, near_ref, None, row, count, lanes)

        rows = (*range(RATE), *range(count - RATE, count))
        total, squares = dilated_rows(row_at, rows, taps_of(filter_ref, lanes), out_ref, lanes)
        store_sums(sums_ref, lanes, total, squares)
        sums_ref[:, lanes] = sums_ref[:, lanes] + inner_ref[:, lanes]


def outer_body(x_ref, chip_ref, near_ref, far_ref, filter_ref, out_ref):
    count = x_ref.shape[0]

    @pl.loop(0, x_ref.shape[2] // LANES)
    def _(block):
        lanes = pl.ds(pl.multiple_of(block * LANES, LANES), LANES)
        taps = taps_of(filter_ref, lanes)

        @functools.cache
        def row_at(row):
            if 0 <= row < count:
                return x_ref[row, :, lanes].astype(jnp.float32)
            return halo_row(chip_ref, near_ref, far_ref, row, count, lanes)

        for place, row in enumerate((*range(-RATE, 0), *range(count, count + RATE))):
            rows = [row_at(row - RATE), row_at(row), row_at(row + RATE)]
            out_ref[place, :, lanes] = dilated_row(rows, taps)


def store_terms(terms_ref, parts_ref, gain_ref, shift_ref, pixels):
    for block in range(gain_ref.shape[0]):
        lanes = slice(block * LANES, (block + 1) * LANES)
        sums = jnp.sum(parts_ref[:, :, lanes], axis=0)
        average = sums[0:1] / pixels
        variance = sums[1:2] / pixels - average * average
        factor = gain_ref[block : block + 1] * lax.rsqrt(variance + epsilon)
        terms_ref[0:1, lanes] = factor
        terms_ref[1:2, lanes] = shift_ref[block : block + 1] - average * factor


def third_body(
    pixels, u_ref, outer_ref, parts_ref, gain_ref, shift_ref, filter_ref,
    weight_hbm, out_ref, sums_ref, weight_ref, terms_ref, arrived,
):
    count = u_ref.shape[0]
    weight_copy = pltpu.make_async_copy(weight_hbm, weight_ref, arrived)
    weight_copy.start()
    store_terms(terms_ref, parts_ref, gain_ref, shift_ref, pixels)

    @pl.loop(0, u_ref.shape[2] // LANES)
    def _(block):
        lanes = pl.ds(pl.multiple_of(block * LANES, LANES), LANES)
        taps = taps_of(filter_ref, lanes)
        factor = terms_ref[0:1, lanes]
        offset = terms_ref[1:2, lanes]
        strip = lax.axis_index(SPACE)
        above = (strip > 0).astype(jnp.float32)
        below = (strip < lax.axis_size(SPACE) - 1).astype(jnp.float32)

        @functools.cache
        def row_at(row):
            if row < 0:
                value = outer_ref[row + RATE, :, lanes]
                value = value * (factor * above) + offset * above
            elif row >= count:
                value = outer_ref[row - count + RATE, :, lanes]
                value = value * (factor * below) + offset * below
            else:
                value = u_ref[row, :, lanes] * factor + offset
            return jnp.maximum(value, 0.0).astype(jnp.bfloat16).astype(jnp.float32)

        total, squares = dilated_rows(row_at, range(count), taps, out_ref, lanes)
        store_sums(sums_ref, lanes, total, squares)

    weight_copy.wait()


def project_body(pixels, places, n_parts, *refs):
    part_refs = refs[:n_parts]
    parts_ref, gain_ref, shift_ref, weight_ref, out_ref, sums_ref = refs[n_parts : n_parts + 6]
    terms_ref, act_ref = refs[n_parts + 6 :]
    count, cols, width = out_ref.shape
    depth = act_ref.shape[1]
    wide = 512
    store_terms(terms_ref, parts_ref, gain_ref, shift_ref, pixels)
    pair = 2
    for u_ref, first_row in zip(part_refs, places):

        @pl.loop(0, u_ref.shape[0] // pair)
        def _(step):
            factor = terms_ref[0:1]
            offset = terms_ref[1:2]
            value = u_ref[pl.ds(step * pair, pair)].reshape(pair * cols, depth)
            row = first_row + step * pair
            if len(places) > 1 and first_row == 0:
                row = step * (count - pair)
            act_ref[pl.ds(pl.multiple_of(row * cols, pair * cols), pair * cols)] = jnp.maximum(
                value * factor + offset, 0.0
            ).astype(jnp.bfloat16)

    @pl.loop(0, width // wide)
    def _(block):
        lanes = pl.ds(pl.multiple_of(block * wide, wide), wide)
        result = jnp.dot(act_ref[...], weight_ref[:, lanes], preferred_element_type=jnp.float32)
        store_sums(sums_ref, lanes, summed_rows(result), summed_rows(result * result))
        out_ref[:, :, lanes] = result.reshape(count, cols, wide)


def outer_project_body(pixels, u_ref, parts_ref, gain_ref, shift_ref, weight_ref, out_ref, terms_ref, act_ref):
    count, cols, width = out_ref.shape
    wide = 512
    store_terms(terms_ref, parts_ref, gain_ref, shift_ref, pixels)
    value = u_ref[...].reshape(count * cols, u_ref.shape[2])
    act_ref[...] = jnp.maximum(value * terms_ref[0:1] + terms_ref[1:2], 0.0).astype(jnp.bfloat16)

    @pl.loop(0, width // wide)
    def _(block):
        lanes = pl.ds(pl.multiple_of(block * wide, wide), wide)
        result = jnp.dot(act_ref[...], weight_ref[:, lanes], preferred_element_type=jnp.float32)
        out_ref[:, :, lanes] = result.reshape(count, cols, wide)


def last_body(pixels, u_ref, parts_ref, gain_ref, shift_ref, out_hbm, terms_ref, rows_ref, sent):
    store_terms(terms_ref, parts_ref, gain_ref, shift_ref, pixels)

    def piece(row):
        return pltpu.make_async_copy(rows_ref.at[row], out_hbm.at[0, row], sent.at[row])

    @pl.loop(0, u_ref.shape[0])
    def _(row):
        value = u_ref[row] * terms_ref[0:1] + terms_ref[1:2]
        rows_ref[row] = jnp.maximum(value, 0.0).astype(jnp.bfloat16)
        piece(row).start()

    @pl.loop(0, u_ref.shape[0])
    def _(row):
        piece(row).wait()


def dilated_inner(x, taps, weight):
    rows, cols, depth = x.shape
    inner = rows - 2 * RATE
    return pl.pallas_call(
        inner_body,
        out_shape=[
            pltpu.VMEM((inner, cols, depth), jnp.float32),
            pltpu.VMEM((2, depth), jnp.float32),
            pltpu.VMEM(weight.shape, weight.dtype),
        ],
        in_specs=[VMEM] * 2 + [HBM],
        out_specs=[VMEM] * 3,
        scratch_shapes=[pltpu.SemaphoreType.DMA],
        compiler_params=pltpu.CompilerParams(vmem_limit_bytes=12 << 20),
        cost_estimate=pl.CostEstimate(
            flops=20 * inner * cols * depth, bytes_accessed=6 * rows * cols * depth, transcendentals=0
        ),
    )(x, taps, weight)


def kept_in_hbm(array):
    return pltpu.with_memory_space_constraint(array, pltpu.HBM)


def loaded(x, taps):
    edges = [(count,) + x.shape[2:] for count in (2 * RATE, RATE, RATE)]
    return pl.pallas_call(
        load_body,
        out_shape=[pltpu.VMEM(shape, x.dtype) for shape in (*edges, x.shape[1:], taps.shape)],
        in_specs=[HBM] * 2,
        out_specs=[VMEM] * 5,
        scratch_shapes=[pltpu.SemaphoreType.DMA((5,))],
        compiler_params=pltpu.CompilerParams(vmem_limit_bytes=4 << 20),
    )(x, taps)


def dilated_edges(x, chip, near, weight, inner_sums):
    cols, depth = x.shape[1:]
    return kernel_call(
        edge_body,
        [((2 * RATE, cols, depth), jnp.float32), ((2, depth), jnp.float32)],
        5,
        12 << 20,
        flops=40 * RATE * cols * depth,
        moved=20 * RATE * cols * depth,
    )(x, chip, near, weight, inner_sums)


def project(pixels, pieces, places, parts, gain, shift, weight):
    rows = sum(piece.shape[0] for piece in pieces)
    cols, depth = pieces[0].shape[1:]
    width = weight.shape[1]
    outs = [((rows, cols, width), jnp.float32), ((2, width), jnp.float32)]
    return pl.pallas_call(
        functools.partial(project_body, pixels, places, len(pieces)),
        out_shape=[pltpu.VMEM(shape, dtype) for shape, dtype in outs],
        in_specs=[VMEM] * (len(pieces) + 4),
        out_specs=[VMEM] * len(outs),
        scratch_shapes=[
            pltpu.VMEM((2, depth), jnp.float32),
            pltpu.VMEM((rows * cols, depth), jnp.bfloat16),
        ],
        compiler_params=pltpu.CompilerParams(vmem_limit_bytes=24 << 20),
        cost_estimate=pl.CostEstimate(
            flops=2 * rows * cols * depth * width,
            bytes_accessed=4 * rows * cols * (depth + width) + 2 * depth * width,
            transcendentals=0,
        ),
    )(*pieces, parts, gain, shift, weight)


def dilated_outer(x, chip, near, far, taps):
    cols, depth = x.shape[1:]
    (outer,) = kernel_call(
        outer_body,
        [((2 * RATE, cols, depth), jnp.float32)],
        5,
        8 << 20,
        flops=36 * RATE * cols * depth,
        moved=20 * RATE * cols * depth,
    )(x, chip, near, far, taps)
    return outer


def project_outer(pixels, u, parts, gain, shift, weight):
    rows, cols, depth = u.shape
    width = weight.shape[1]
    (outer,) = kernel_call(
        functools.partial(outer_project_body, pixels),
        [((rows, cols, width), jnp.float32)],
        5,
        12 << 20,
        scratch=[pltpu.VMEM((2, depth), jnp.float32), pltpu.VMEM((rows * cols, depth), jnp.bfloat16)],
        flops=2 * rows * cols * depth * width,
        moved=4 * rows * cols * (depth + width) + 2 * depth * width,
    )(u, parts, gain, shift, weight)
    return outer


def dilated_second(pixels, u, outer, parts, gain, shift, taps, weight):
    rows, cols, depth = u.shape
    return pl.pallas_call(
        functools.partial(third_body, pixels),
        out_shape=[
            pltpu.VMEM((rows, cols, depth), jnp.float32),
            pltpu.VMEM((2, depth), jnp.float32),
            pltpu.VMEM(weight.shape, weight.dtype),
        ],
        in_specs=[VMEM] * 6 + [HBM],
        out_specs=[VMEM] * 3,
        scratch_shapes=[pltpu.VMEM((2, depth), jnp.float32), pltpu.SemaphoreType.DMA],
        compiler_params=pltpu.CompilerParams(vmem_limit_bytes=16 << 20),
        cost_estimate=pl.CostEstimate(
            flops=26 * rows * cols * depth, bytes_accessed=8 * rows * cols * depth, transcendentals=0
        ),
    )(u, outer, parts, gain, shift, taps, weight)


def last_norm(pixels, u, parts, gain, shift):
    rows, cols, depth = u.shape
    return pl.pallas_call(
        functools.partial(last_body, pixels),
        out_shape=jax.ShapeDtypeStruct((1, rows, cols, depth), jnp.bfloat16),
        in_specs=[VMEM] * 4,
        out_specs=HBM,
        scratch_shapes=[
            pltpu.VMEM((2, depth), jnp.float32),
            pltpu.VMEM((rows, cols, depth), jnp.bfloat16),
            pltpu.SemaphoreType.DMA((rows,)),
        ],
        compiler_params=pltpu.CompilerParams(vmem_limit_bytes=16 << 20),
        cost_estimate=pl.CostEstimate(
            flops=3 * rows * cols * depth, bytes_accessed=6 * rows * cols * depth, transcendentals=0
        ),
    )(u, parts, gain, shift)


def pair_body(own_ref, other_ref, out_ref):
    out_ref[...] = jnp.broadcast_to((own_ref[...] + other_ref[...])[None], out_ref.shape)


def group_body(parts_ref, out_ref):
    out_ref[...] = jnp.broadcast_to(jnp.sum(parts_ref[...], axis=0)[None], out_ref.shape)


def gathered_sums(value, beside=None):
    plane, line = ("batch_1", "space_0"), ("batch_0",)
    other = lax.ppermute(value, "space_1", [(0, 1), (1, 0)])
    if beside is not None:
        other, beside = lax.optimization_barrier((other, beside))
    shape = (lax.axis_size(plane),) + value.shape
    (copies,) = kernel_call(pair_body, [(shape, jnp.float32)], 2, 2 << 20)(value, other)
    parts = lax.all_to_all(copies, plane, 0, 0)
    shape = (lax.axis_size(line),) + value.shape
    (copies,) = kernel_call(group_body, [(shape, jnp.float32)], 1, 2 << 20)(parts)
    return lax.all_to_all(copies, line, 0, 0), beside


def from_neighbours(chip, near, far):
    ends = [pair for i in range(1, lax.axis_size(SPACE) - 1, 2) for pair in ((i, i + 1), (i + 1, i))]
    near = lax.ppermute(near, SPACE, ends)
    chip = lax.ppermute(chip, "space_1", [(0, 1), (1, 0)])
    return chip, near, lax.ppermute(far, SPACE, ends)


def per_device(
    features,
    depth_one,
    gain_one,
    shift_one,
    point_one,
    gain_two,
    shift_two,
    depth_two,
    gain_three,
    shift_three,
    point_two,
    gain_four,
    shift_four,
):
    rows, cols = features.shape[1:3]
    pixels = rows * cols * lax.axis_size(BATCH) * lax.axis_size(SPACE)
    names = (gain_one, shift_one, gain_two, shift_two, gain_three, shift_three, gain_four, shift_four)
    terms = [term.reshape(-1, LANES) for term in names]
    chip, near, far, x, taps = loaded(kept_in_hbm(features), kept_in_hbm(depth_one))
    chip, near, far = from_neighbours(chip, near, far)
    inner, inner_sums, weight = dilated_inner(x, taps, kept_in_hbm(point_one))
    edges, sums = dilated_edges(x, chip, near, taps, inner_sums)
    parts, outer = gathered_sums(sums, dilated_outer(x, chip, near, far, taps))
    second, sums = project(pixels, (edges, inner), (0, RATE), parts, *terms[0:2], weight)
    outer = project_outer(pixels, outer, parts, *terms[0:2], weight)
    parts, outer = gathered_sums(sums, outer)
    third, sums, weight = dilated_second(
        pixels, second, outer, parts, *terms[2:4], depth_two, kept_in_hbm(point_two)
    )
    parts, _ = gathered_sums(sums)
    fourth, sums = project(pixels, (third,), (0,), parts, *terms[4:6], weight)
    parts, _ = gathered_sums(sums)
    return last_norm(pixels, fourth, parts, *terms[6:8])


def solution(mesh):
    finer = Mesh(mesh.devices.reshape(8, 4, 4, 2), ("batch_0", "batch_1", "space_0", "space_1"))
    placed = (P(BATCH, SPACE, None, None),) + (P(),) * 12
    return jax.shard_map(
        per_device,
        mesh=finer,
        in_specs=placed,
        out_specs=P(BATCH, SPACE, None, None),
        check_vma=False,
    )
```

```python
import functools

import jax
import jax.numpy as jnp
from jax import lax
from jax.experimental import pallas as pl
from jax.experimental.pallas import tpu as pltpu
from jax.sharding import Mesh
from jax.sharding import PartitionSpec as P

RATE = 2
LANES = 128
PAD = 8
BATCH = ("batch_0", "batch_1")
SPACE = ("space_0", "space_1")

epsilon = 1e-05

VMEM = pl.BlockSpec(memory_space=pltpu.VMEM)
HBM = pl.BlockSpec(memory_space=pltpu.HBM)


def kernel_call(body, outs, n_in, limit, scratch=(), flops=0, moved=0):
    return pl.pallas_call(
        body,
        out_shape=[pltpu.VMEM(shape, dtype) for shape, dtype in outs],
        in_specs=[VMEM] * n_in,
        out_specs=[VMEM] * len(outs),
        scratch_shapes=list(scratch),
        compiler_params=pltpu.CompilerParams(vmem_limit_bytes=limit),
        cost_estimate=pl.CostEstimate(flops=flops, bytes_accessed=moved, transcendentals=0),
    )


def moved_down(row):
    gap = jnp.zeros((RATE, row.shape[1]), row.dtype)
    return jnp.concatenate([gap, row[: row.shape[0] - RATE]], axis=0)


def moved_up(row):
    gap = jnp.zeros((RATE, row.shape[1]), row.dtype)
    return jnp.concatenate([row[RATE:], gap], axis=0)


def taps_of(filter_ref, lanes):
    return [filter_ref[tap, :, lanes].astype(jnp.float32) for tap in range(3)]


def dilated_row(rows, taps):
    sides = []
    for tap_col in range(3):
        side = None
        for tap_row in range(3):
            term = rows[tap_row] * taps[tap_row][tap_col : tap_col + 1]
            side = term if side is None else side + term
        sides.append(side)
    return sides[1] + moved_down(sides[0]) + moved_up(sides[2])


def summed_rows(value):
    return jnp.sum(value.reshape(value.shape[0] // 8, 8, value.shape[1]), axis=0)


def store_sums(sums_ref, lanes, total, squares):
    sums_ref[0:1, lanes] = jnp.sum(total, axis=0, keepdims=True)
    sums_ref[1:2, lanes] = jnp.sum(squares, axis=0, keepdims=True)


def dilated_rows(row_at, rows, taps, out_ref, lanes):
    total = squares = None
    for place, row in sorted(enumerate(rows), key=lambda pair: (pair[1] % 2, pair[1])):
        value = dilated_row([row_at(row - RATE), row_at(row), row_at(row + RATE)], taps)
        out_ref[place, :, lanes] = value
        part, part_squares = summed_rows(value), summed_rows(value * value)
        total = part if total is None else total + part
        squares = part_squares if squares is None else squares + part_squares
    return total, squares


def inner_body(
    x_hbm, filter_hbm, weight_hbm, out_ref, sums_ref, x_ref, filter_ref, weight_ref, arrived,
    filter_arrived, weight_arrived,
):
    count, _, depth = x_ref.shape
    wide = depth // arrived.shape[0]

    def piece(place):
        lanes = pl.ds(place * wide, wide)
        return pltpu.make_async_copy(
            x_hbm.at[0, :, :, lanes], x_ref.at[:, :, lanes], arrived.at[place]
        )

    taps_copy = pltpu.make_async_copy(filter_hbm, filter_ref, filter_arrived)
    taps_copy.start()
    for place in range(arrived.shape[0]):
        piece(place).start()
    weight_copy = pltpu.make_async_copy(weight_hbm, weight_ref, weight_arrived)
    weight_copy.start()
    taps_copy.wait()
    for place in range(arrived.shape[0]):
        piece(place).wait()

        @pl.loop(place * wide // LANES, (place + 1) * wide // LANES)
        def _(block):
            lanes = pl.ds(pl.multiple_of(block * LANES, LANES), LANES)
            total, squares = dilated_rows(
                functools.cache(lambda row: x_ref[row, :, lanes].astype(jnp.float32)),
                range(RATE, count - RATE),
                taps_of(filter_ref, lanes),
                out_ref,
                lanes,
            )
            store_sums(sums_ref, lanes, total, squares)

    weight_copy.wait()


def edge_starts(count):
    core = lax.axis_index("space_1")
    return (
        (1 - core) * (count - 2 * RATE),
        core * (count - RATE),
        RATE + core * (count - 3 * RATE),
    )


def load_body(x_hbm, chip_ref, near_ref, far_ref, arrived):
    starts = edge_starts(x_hbm.shape[1])
    copies = [
        pltpu.make_async_copy(
            x_hbm.at[0, pl.ds(start, out_ref.shape[0])], out_ref, arrived.at[place]
        )
        for place, (start, out_ref) in enumerate(zip(starts, (chip_ref, near_ref, far_ref)))
    ]
    for copy in copies:
        copy.start()
    for copy in copies:
        copy.wait()


def halo_row(chip_ref, near_ref, far_ref, row, count, lanes):
    core = lax.axis_index("space_1")
    if row < 0:
        chip_holds, chip_row = core == 1, row + 2 * RATE
        cross_ref, cross_row = (near_ref, row + RATE) if row >= -RATE else (far_ref, row + 2 * RATE)
    else:
        chip_holds, chip_row = core == 0, row - count
        cross_ref, cross_row = (
            (near_ref, row - count) if row < count + RATE else (far_ref, row - count - RATE)
        )
    value = jnp.where(chip_holds, chip_ref[chip_row, :, lanes], cross_ref[cross_row, :, lanes])
    return value.astype(jnp.float32)


def edge_body(x_ref, chip_ref, near_ref, filter_ref, inner_ref, out_ref, sums_ref):
    count = x_ref.shape[0]

    @pl.loop(0, x_ref.shape[2] // LANES)
    def _(block):
        lanes = pl.ds(pl.multiple_of(block * LANES, LANES), LANES)

        @functools.cache
        def row_at(row):
            if 0 <= row < count:
                return x_ref[row, :, lanes].astype(jnp.float32)
            return halo_row(chip_ref, near_ref, None, row, count, lanes)

        rows = (*range(RATE), *range(count - RATE, count))
        total, squares = dilated_rows(row_at, rows, taps_of(filter_ref, lanes), out_ref, lanes)
        store_sums(sums_ref, lanes, total, squares)
        sums_ref[:, lanes] = sums_ref[:, lanes] + inner_ref[:, lanes]


def outer_body(x_ref, chip_ref, near_ref, far_ref, filter_ref, out_ref):
    count = x_ref.shape[0]

    @pl.loop(0, x_ref.shape[2] // LANES)
    def _(block):
        lanes = pl.ds(pl.multiple_of(block * LANES, LANES), LANES)
        taps = taps_of(filter_ref, lanes)

        @functools.cache
        def row_at(row):
            if 0 <= row < count:
                return x_ref[row, :, lanes].astype(jnp.float32)
            return halo_row(chip_ref, near_ref, far_ref, row, count, lanes)

        for place, row in enumerate((*range(-RATE, 0), *range(count, count + RATE))):
            rows = [row_at(row - RATE), row_at(row), row_at(row + RATE)]
            out_ref[place, :, lanes] = dilated_row(rows, taps)


def store_terms(terms_ref, parts_ref, gain_ref, shift_ref, pixels):
    for block in range(gain_ref.shape[0]):
        lanes = slice(block * LANES, (block + 1) * LANES)
        sums = jnp.sum(parts_ref[:, :, lanes], axis=0)
        average = sums[0:1] / pixels
        variance = sums[1:2] / pixels - average * average
        factor = gain_ref[block : block + 1] * lax.rsqrt(variance + epsilon)
        terms_ref[0:1, lanes] = factor
        terms_ref[1:2, lanes] = shift_ref[block : block + 1] - average * factor


def third_body(
    pixels, u_ref, outer_ref, parts_ref, gain_ref, shift_ref, filter_ref,
    weight_hbm, out_ref, sums_ref, weight_ref, terms_ref, padded_ref, arrived,
):
    count = u_ref.shape[0]
    weight_copy = pltpu.make_async_copy(weight_hbm, weight_ref, arrived)
    weight_copy.start()
    store_terms(terms_ref, parts_ref, gain_ref, shift_ref, pixels)
    cols = u_ref.shape[1]
    gap = jnp.zeros((count + 2 * RATE, PAD, LANES), jnp.float32)
    padded_ref[:, :PAD] = gap
    padded_ref[:, PAD + cols :] = gap

    @pl.loop(0, u_ref.shape[2] // LANES)
    def _(block):
        lanes = pl.ds(pl.multiple_of(block * LANES, LANES), LANES)
        taps = taps_of(filter_ref, lanes)
        factor = terms_ref[0:1, lanes]
        offset = terms_ref[1:2, lanes]
        strip = lax.axis_index(SPACE)
        above = (strip > 0).astype(jnp.float32)
        below = (strip < lax.axis_size(SPACE) - 1).astype(jnp.float32)

        def row_at(row):
            if row < 0:
                value = outer_ref[row + RATE, :, lanes]
                value = value * (factor * above) + offset * above
            elif row >= count:
                value = outer_ref[row - count + RATE, :, lanes]
                value = value * (factor * below) + offset * below
            else:
                value = u_ref[row, :, lanes] * factor + offset
            return jnp.maximum(value, 0.0).astype(jnp.bfloat16).astype(jnp.float32)

        for row in range(-RATE, count + RATE):
            padded_ref[row + RATE, PAD : PAD + cols] = row_at(row)
        total = squares = 0.0
        for row in range(count):
            value = None
            for tap_row in range(3):
                for tap_col in range(3):
                    first_col = PAD + (tap_col - 1) * RATE
                    term = padded_ref[row + tap_row * RATE, first_col : first_col + cols]
                    term = term * taps[tap_row][tap_col : tap_col + 1]
                    value = term if value is None else value + term
            out_ref[row, :, lanes] = value
            total = total + summed_rows(value)
            squares = squares + summed_rows(value * value)
        store_sums(sums_ref, lanes, total, squares)

    weight_copy.wait()


def project_body(pixels, places, n_parts, *refs):
    part_refs = refs[:n_parts]
    parts_ref, gain_ref, shift_ref, weight_ref, out_ref, sums_ref = refs[n_parts : n_parts + 6]
    terms_ref, act_ref = refs[n_parts + 6 :]
    count, cols, width = out_ref.shape
    depth = act_ref.shape[1]
    wide = 512
    store_terms(terms_ref, parts_ref, gain_ref, shift_ref, pixels)
    pair = 2
    for u_ref, first_row in zip(part_refs, places):

        @pl.loop(0, u_ref.shape[0] // pair)
        def _(step):
            factor = terms_ref[0:1]
            offset = terms_ref[1:2]
            value = u_ref[pl.ds(step * pair, pair)].reshape(pair * cols, depth)
            row = first_row + step * pair
            if len(places) > 1 and first_row == 0:
                row = step * (count - pair)
            act_ref[pl.ds(pl.multiple_of(row * cols, pair * cols), pair * cols)] = jnp.maximum(
                value * factor + offset, 0.0
            ).astype(jnp.bfloat16)

    @pl.loop(0, width // wide)
    def _(block):
        lanes = pl.ds(pl.multiple_of(block * wide, wide), wide)
        result = jnp.dot(act_ref[...], weight_ref[:, lanes], preferred_element_type=jnp.float32)
        store_sums(sums_ref, lanes, summed_rows(result), summed_rows(result * result))
        out_ref[:, :, lanes] = result.reshape(count, cols, wide)


def outer_project_body(pixels, u_ref, parts_ref, gain_ref, shift_ref, weight_ref, out_ref, terms_ref, act_ref):
    count, cols, width = out_ref.shape
    wide = 512
    store_terms(terms_ref, parts_ref, gain_ref, shift_ref, pixels)
    value = u_ref[...].reshape(count * cols, u_ref.shape[2])
    act_ref[...] = jnp.maximum(value * terms_ref[0:1] + terms_ref[1:2], 0.0).astype(jnp.bfloat16)

    @pl.loop(0, width // wide)
    def _(block):
        lanes = pl.ds(pl.multiple_of(block * wide, wide), wide)
        result = jnp.dot(act_ref[...], weight_ref[:, lanes], preferred_element_type=jnp.float32)
        out_ref[:, :, lanes] = result.reshape(count, cols, wide)


def last_body(pixels, u_ref, parts_ref, gain_ref, shift_ref, out_hbm, terms_ref, rows_ref, sent):
    store_terms(terms_ref, parts_ref, gain_ref, shift_ref, pixels)

    def piece(row):
        return pltpu.make_async_copy(rows_ref.at[row], out_hbm.at[0, row], sent.at[row])

    @pl.loop(0, u_ref.shape[0])
    def _(row):
        value = u_ref[row] * terms_ref[0:1] + terms_ref[1:2]
        rows_ref[row] = jnp.maximum(value, 0.0).astype(jnp.bfloat16)
        piece(row).start()

    @pl.loop(0, u_ref.shape[0])
    def _(row):
        piece(row).wait()


def dilated_inner(x, taps, weight):
    rows, cols, depth = x.shape[1:]
    inner = rows - 2 * RATE
    return pl.pallas_call(
        inner_body,
        out_shape=[
            pltpu.VMEM((inner, cols, depth), jnp.float32),
            pltpu.VMEM((2, depth), jnp.float32),
            pltpu.VMEM((rows, cols, depth), x.dtype),
            pltpu.VMEM(taps.shape, taps.dtype),
            pltpu.VMEM(weight.shape, weight.dtype),
        ],
        in_specs=[HBM] * 3,
        out_specs=[VMEM] * 5,
        scratch_shapes=[pltpu.SemaphoreType.DMA((4,))] + [pltpu.SemaphoreType.DMA] * 2,
        compiler_params=pltpu.CompilerParams(vmem_limit_bytes=12 << 20),
        cost_estimate=pl.CostEstimate(
            flops=20 * inner * cols * depth, bytes_accessed=6 * rows * cols * depth, transcendentals=0
        ),
    )(x, taps, weight)


def kept_in_hbm(array):
    return pltpu.with_memory_space_constraint(array, pltpu.HBM)


def edge_rows(x):
    edges = [(count,) + x.shape[2:] for count in (2 * RATE, RATE, RATE)]
    return pl.pallas_call(
        load_body,
        out_shape=[pltpu.VMEM(shape, x.dtype) for shape in edges],
        in_specs=[HBM],
        out_specs=[VMEM] * 3,
        scratch_shapes=[pltpu.SemaphoreType.DMA((3,))],
        compiler_params=pltpu.CompilerParams(vmem_limit_bytes=4 << 20),
    )(x)


def dilated_edges(x, chip, near, weight, inner_sums):
    cols, depth = x.shape[1:]
    return kernel_call(
        edge_body,
        [((2 * RATE, cols, depth), jnp.float32), ((2, depth), jnp.float32)],
        5,
        12 << 20,
        flops=40 * RATE * cols * depth,
        moved=20 * RATE * cols * depth,
    )(x, chip, near, weight, inner_sums)


def project(pixels, pieces, places, parts, gain, shift, weight):
    rows = sum(piece.shape[0] for piece in pieces)
    cols, depth = pieces[0].shape[1:]
    width = weight.shape[1]
    outs = [((rows, cols, width), jnp.float32), ((2, width), jnp.float32)]
    return pl.pallas_call(
        functools.partial(project_body, pixels, places, len(pieces)),
        out_shape=[pltpu.VMEM(shape, dtype) for shape, dtype in outs],
        in_specs=[VMEM] * (len(pieces) + 4),
        out_specs=[VMEM] * len(outs),
        scratch_shapes=[
            pltpu.VMEM((2, depth), jnp.float32),
            pltpu.VMEM((rows * cols, depth), jnp.bfloat16),
        ],
        compiler_params=pltpu.CompilerParams(vmem_limit_bytes=24 << 20),
        cost_estimate=pl.CostEstimate(
            flops=2 * rows * cols * depth * width,
            bytes_accessed=4 * rows * cols * (depth + width) + 2 * depth * width,
            transcendentals=0,
        ),
    )(*pieces, parts, gain, shift, weight)


def dilated_outer(x, chip, near, far, taps):
    cols, depth = x.shape[1:]
    (outer,) = kernel_call(
        outer_body,
        [((2 * RATE, cols, depth), jnp.float32)],
        5,
        8 << 20,
        flops=36 * RATE * cols * depth,
        moved=20 * RATE * cols * depth,
    )(x, chip, near, far, taps)
    return outer


def project_outer(pixels, u, parts, gain, shift, weight):
    rows, cols, depth = u.shape
    width = weight.shape[1]
    (outer,) = kernel_call(
        functools.partial(outer_project_body, pixels),
        [((rows, cols, width), jnp.float32)],
        5,
        12 << 20,
        scratch=[pltpu.VMEM((2, depth), jnp.float32), pltpu.VMEM((rows * cols, depth), jnp.bfloat16)],
        flops=2 * rows * cols * depth * width,
        moved=4 * rows * cols * (depth + width) + 2 * depth * width,
    )(u, parts, gain, shift, weight)
    return outer


def dilated_second(pixels, u, outer, parts, gain, shift, taps, weight):
    rows, cols, depth = u.shape
    return pl.pallas_call(
        functools.partial(third_body, pixels),
        out_shape=[
            pltpu.VMEM((rows, cols, depth), jnp.float32),
            pltpu.VMEM((2, depth), jnp.float32),
            pltpu.VMEM(weight.shape, weight.dtype),
        ],
        in_specs=[VMEM] * 6 + [HBM],
        out_specs=[VMEM] * 3,
        scratch_shapes=[
            pltpu.VMEM((2, depth), jnp.float32),
            pltpu.VMEM((rows + 2 * RATE, cols + 2 * PAD, LANES), jnp.float32),
            pltpu.SemaphoreType.DMA,
        ],
        compiler_params=pltpu.CompilerParams(vmem_limit_bytes=16 << 20),
        cost_estimate=pl.CostEstimate(
            flops=26 * rows * cols * depth, bytes_accessed=8 * rows * cols * depth, transcendentals=0
        ),
    )(u, outer, parts, gain, shift, taps, weight)


def last_norm(pixels, u, parts, gain, shift):
    rows, cols, depth = u.shape
    return pl.pallas_call(
        functools.partial(last_body, pixels),
        out_shape=jax.ShapeDtypeStruct((1, rows, cols, depth), jnp.bfloat16),
        in_specs=[VMEM] * 4,
        out_specs=HBM,
        scratch_shapes=[
            pltpu.VMEM((2, depth), jnp.float32),
            pltpu.VMEM((rows, cols, depth), jnp.bfloat16),
            pltpu.SemaphoreType.DMA((rows,)),
        ],
        compiler_params=pltpu.CompilerParams(vmem_limit_bytes=16 << 20),
        cost_estimate=pl.CostEstimate(
            flops=3 * rows * cols * depth, bytes_accessed=6 * rows * cols * depth, transcendentals=0
        ),
    )(u, parts, gain, shift)


def pair_body(own_ref, other_ref, out_ref):
    out_ref[...] = jnp.broadcast_to((own_ref[...] + other_ref[...])[None], out_ref.shape)


def group_body(parts_ref, out_ref):
    out_ref[...] = jnp.broadcast_to(jnp.sum(parts_ref[...], axis=0)[None], out_ref.shape)


def gathered_sums(value, beside=None):
    plane, line = ("batch_1", "space_0"), ("batch_0",)
    other = lax.ppermute(value, "space_1", [(0, 1), (1, 0)])
    if beside is not None:
        other, beside = lax.optimization_barrier((other, beside))
    shape = (lax.axis_size(plane),) + value.shape
    (copies,) = kernel_call(pair_body, [(shape, jnp.float32)], 2, 2 << 20)(value, other)
    parts = lax.all_to_all(copies, plane, 0, 0)
    shape = (lax.axis_size(line),) + value.shape
    (copies,) = kernel_call(group_body, [(shape, jnp.float32)], 1, 2 << 20)(parts)
    return lax.all_to_all(copies, line, 0, 0), beside


def from_neighbours(chip, near, far):
    ends = [pair for i in range(1, lax.axis_size(SPACE) - 1, 2) for pair in ((i, i + 1), (i + 1, i))]
    near = lax.ppermute(near, SPACE, ends)
    chip = lax.ppermute(chip, "space_1", [(0, 1), (1, 0)])
    return chip, near, lax.ppermute(far, SPACE, ends)


def per_device(
    features,
    depth_one,
    gain_one,
    shift_one,
    point_one,
    gain_two,
    shift_two,
    depth_two,
    gain_three,
    shift_three,
    point_two,
    gain_four,
    shift_four,
):
    rows, cols = features.shape[1:3]
    pixels = rows * cols * lax.axis_size(BATCH) * lax.axis_size(SPACE)
    names = (gain_one, shift_one, gain_two, shift_two, gain_three, shift_three, gain_four, shift_four)
    terms = [term.reshape(-1, LANES) for term in names]
    features = kept_in_hbm(features)
    chip, near, far = from_neighbours(*edge_rows(features))
    inner, inner_sums, x, taps, weight = dilated_inner(
        features, kept_in_hbm(depth_one), kept_in_hbm(point_one)
    )
    edges, sums = dilated_edges(x, chip, near, taps, inner_sums)
    parts, outer = gathered_sums(sums, dilated_outer(x, chip, near, far, taps))
    second, sums = project(pixels, (edges, inner), (0, RATE), parts, *terms[0:2], weight)
    outer = project_outer(pixels, outer, parts, *terms[0:2], weight)
    parts, outer = gathered_sums(sums, outer)
    third, sums, weight = dilated_second(
        pixels, second, outer, parts, *terms[2:4], depth_two, kept_in_hbm(point_two)
    )
    parts, _ = gathered_sums(sums)
    fourth, sums = project(pixels, (third,), (0,), parts, *terms[4:6], weight)
    parts, _ = gathered_sums(sums)
    return last_norm(pixels, fourth, parts, *terms[6:8])


def solution(mesh):
    finer = Mesh(mesh.devices.reshape(8, 4, 4, 2), ("batch_0", "batch_1", "space_0", "space_1"))
    placed = (P(BATCH, SPACE, None, None),) + (P(),) * 12
    return jax.shard_map(
        per_device,
        mesh=finer,
        in_specs=placed,
        out_specs=P(BATCH, SPACE, None, None),
        check_vma=False,
    )
```

```python
import functools

import jax
import jax.numpy as jnp
from jax import lax
from jax.experimental import pallas as pl
from jax.experimental.pallas import tpu as pltpu
from jax.sharding import Mesh
from jax.sharding import PartitionSpec as P

RATE = 2
LANES = 128
PAD = 8
BATCH = ("batch_0", "batch_1")
SPACE = ("space_0", "space_1")

epsilon = 1e-05

VMEM = pl.BlockSpec(memory_space=pltpu.VMEM)
HBM = pl.BlockSpec(memory_space=pltpu.HBM)


def kernel_call(body, outs, n_in, limit, scratch=(), flops=0, moved=0):
    return pl.pallas_call(
        body,
        out_shape=[pltpu.VMEM(shape, dtype) for shape, dtype in outs],
        in_specs=[VMEM] * n_in,
        out_specs=[VMEM] * len(outs),
        scratch_shapes=list(scratch),
        compiler_params=pltpu.CompilerParams(vmem_limit_bytes=limit),
        cost_estimate=pl.CostEstimate(flops=flops, bytes_accessed=moved, transcendentals=0),
    )


def moved_down(row):
    gap = jnp.zeros((RATE, row.shape[1]), row.dtype)
    return jnp.concatenate([gap, row[: row.shape[0] - RATE]], axis=0)


def moved_up(row):
    gap = jnp.zeros((RATE, row.shape[1]), row.dtype)
    return jnp.concatenate([row[RATE:], gap], axis=0)


def taps_of(filter_ref, lanes):
    return [filter_ref[tap, :, lanes].astype(jnp.float32) for tap in range(3)]


def dilated_row(rows, taps):
    sides = []
    for tap_col in range(3):
        side = None
        for tap_row in range(3):
            term = rows[tap_row] * taps[tap_row][tap_col : tap_col + 1]
            side = term if side is None else side + term
        sides.append(side)
    return sides[1] + moved_down(sides[0]) + moved_up(sides[2])


def summed_rows(value):
    return jnp.sum(value.reshape(value.shape[0] // 8, 8, value.shape[1]), axis=0)


def store_sums(sums_ref, lanes, total, squares):
    sums_ref[0:1, lanes] = jnp.sum(total, axis=0, keepdims=True)
    sums_ref[1:2, lanes] = jnp.sum(squares, axis=0, keepdims=True)


def dilated_rows(row_at, rows, taps, out_ref, lanes):
    total = squares = None
    for place, row in sorted(enumerate(rows), key=lambda pair: (pair[1] % 2, pair[1])):
        value = dilated_row([row_at(row - RATE), row_at(row), row_at(row + RATE)], taps)
        out_ref[place, :, lanes] = value
        part, part_squares = summed_rows(value), summed_rows(value * value)
        total = part if total is None else total + part
        squares = part_squares if squares is None else squares + part_squares
    return total, squares


def inner_body(
    x_hbm, filter_hbm, weight_hbm, out_ref, sums_ref, x_ref, filter_ref, weight_ref, arrived,
    filter_arrived, weight_arrived,
):
    count, _, depth = x_ref.shape
    wide = depth // arrived.shape[0]

    def piece(place):
        lanes = pl.ds(place * wide, wide)
        return pltpu.make_async_copy(
            x_hbm.at[0, :, :, lanes], x_ref.at[:, :, lanes], arrived.at[place]
        )

    taps_copy = pltpu.make_async_copy(filter_hbm, filter_ref, filter_arrived)
    taps_copy.start()
    for place in range(arrived.shape[0]):
        piece(place).start()
    weight_copy = pltpu.make_async_copy(weight_hbm, weight_ref, weight_arrived)
    weight_copy.start()
    taps_copy.wait()
    for place in range(arrived.shape[0]):
        piece(place).wait()

        @pl.loop(place * wide // LANES, (place + 1) * wide // LANES)
        def _(block):
            lanes = pl.ds(pl.multiple_of(block * LANES, LANES), LANES)
            total, squares = dilated_rows(
                functools.cache(lambda row: x_ref[row, :, lanes].astype(jnp.float32)),
                range(RATE, count - RATE),
                taps_of(filter_ref, lanes),
                out_ref,
                lanes,
            )
            store_sums(sums_ref, lanes, total, squares)

    weight_copy.wait()


def edge_starts(count):
    core = lax.axis_index("space_1")
    return (
        (1 - core) * (count - 2 * RATE),
        core * (count - RATE),
        RATE + core * (count - 3 * RATE),
    )


def load_body(x_hbm, chip_ref, near_ref, far_ref, arrived):
    starts = edge_starts(x_hbm.shape[1])
    copies = [
        pltpu.make_async_copy(
            x_hbm.at[0, pl.ds(start, out_ref.shape[0])], out_ref, arrived.at[place]
        )
        for place, (start, out_ref) in enumerate(zip(starts, (chip_ref, near_ref, far_ref)))
    ]
    for copy in copies:
        copy.start()
    for copy in copies:
        copy.wait()


def halo_row(chip_ref, near_ref, far_ref, row, count, lanes):
    core = lax.axis_index("space_1")
    if row < 0:
        chip_holds, chip_row = core == 1, row + 2 * RATE
        cross_ref, cross_row = (near_ref, row + RATE) if row >= -RATE else (far_ref, row + 2 * RATE)
    else:
        chip_holds, chip_row = core == 0, row - count
        cross_ref, cross_row = (
            (near_ref, row - count) if row < count + RATE else (far_ref, row - count - RATE)
        )
    value = jnp.where(chip_holds, chip_ref[chip_row, :, lanes], cross_ref[cross_row, :, lanes])
    return value.astype(jnp.float32)


def edge_body(x_ref, chip_ref, near_ref, filter_ref, inner_ref, out_ref, sums_ref):
    count = x_ref.shape[0]

    @pl.loop(0, x_ref.shape[2] // LANES)
    def _(block):
        lanes = pl.ds(pl.multiple_of(block * LANES, LANES), LANES)

        @functools.cache
        def row_at(row):
            if 0 <= row < count:
                return x_ref[row, :, lanes].astype(jnp.float32)
            return halo_row(chip_ref, near_ref, None, row, count, lanes)

        rows = (*range(RATE), *range(count - RATE, count))
        total, squares = dilated_rows(row_at, rows, taps_of(filter_ref, lanes), out_ref, lanes)
        store_sums(sums_ref, lanes, total, squares)
        sums_ref[:, lanes] = sums_ref[:, lanes] + inner_ref[:, lanes]


def outer_body(x_ref, chip_ref, near_ref, far_ref, filter_ref, out_ref):
    count = x_ref.shape[0]

    @pl.loop(0, x_ref.shape[2] // LANES)
    def _(block):
        lanes = pl.ds(pl.multiple_of(block * LANES, LANES), LANES)
        taps = taps_of(filter_ref, lanes)

        @functools.cache
        def row_at(row):
            if 0 <= row < count:
                return x_ref[row, :, lanes].astype(jnp.float32)
            return halo_row(chip_ref, near_ref, far_ref, row, count, lanes)

        for place, row in enumerate((*range(-RATE, 0), *range(count, count + RATE))):
            rows = [row_at(row - RATE), row_at(row), row_at(row + RATE)]
            out_ref[place, :, lanes] = dilated_row(rows, taps)


def store_terms(terms_ref, parts_ref, gain_ref, shift_ref, pixels):
    for block in range(gain_ref.shape[0]):
        lanes = slice(block * LANES, (block + 1) * LANES)
        sums = jnp.sum(parts_ref[:, :, lanes], axis=0)
        average = sums[0:1] / pixels
        variance = sums[1:2] / pixels - average * average
        factor = gain_ref[block : block + 1] * lax.rsqrt(variance + epsilon)
        terms_ref[0:1, lanes] = factor
        terms_ref[1:2, lanes] = shift_ref[block : block + 1] - average * factor


def third_body(
    pixels, u_ref, outer_ref, parts_ref, gain_ref, shift_ref, filter_ref,
    weight_hbm, out_ref, sums_ref, weight_ref, terms_ref, padded_ref, arrived,
):
    count = u_ref.shape[0]
    weight_copy = pltpu.make_async_copy(weight_hbm, weight_ref, arrived)
    weight_copy.start()
    store_terms(terms_ref, parts_ref, gain_ref, shift_ref, pixels)
    cols = u_ref.shape[1]
    gap = jnp.zeros((count + 2 * RATE, PAD, LANES), jnp.float32)
    padded_ref[:, :PAD] = gap
    padded_ref[:, PAD + cols :] = gap

    @pl.loop(0, u_ref.shape[2] // LANES)
    def _(block):
        lanes = pl.ds(pl.multiple_of(block * LANES, LANES), LANES)
        taps = taps_of(filter_ref, lanes)
        factor = terms_ref[0:1, lanes]
        offset = terms_ref[1:2, lanes]
        strip = lax.axis_index(SPACE)
        above = (strip > 0).astype(jnp.float32)
        below = (strip < lax.axis_size(SPACE) - 1).astype(jnp.float32)

        def row_at(row):
            if row < 0:
                value = outer_ref[row + RATE, :, lanes]
                value = value * (factor * above) + offset * above
            elif row >= count:
                value = outer_ref[row - count + RATE, :, lanes]
                value = value * (factor * below) + offset * below
            else:
                value = u_ref[row, :, lanes] * factor + offset
            return jnp.maximum(value, 0.0).astype(jnp.bfloat16).astype(jnp.float32)

        for row in range(-RATE, count + RATE):
            padded_ref[row + RATE, PAD : PAD + cols] = row_at(row)
        total = squares = 0.0
        for row in range(count):
            value = None
            for tap_row in range(3):
                for tap_col in range(3):
                    first_col = PAD + (tap_col - 1) * RATE
                    term = padded_ref[row + tap_row * RATE, first_col : first_col + cols]
                    term = term * taps[tap_row][tap_col : tap_col + 1]
                    value = term if value is None else value + term
            out_ref[row, :, lanes] = value
            total = total + summed_rows(value)
            squares = squares + summed_rows(value * value)
        store_sums(sums_ref, lanes, total, squares)

    weight_copy.wait()


def project_body(pixels, blocks, n_parts, *refs):
    part_refs = refs[:n_parts]
    parts_ref, gain_ref, shift_ref, weight_ref, out_ref, sums_ref = refs[n_parts : n_parts + 6]
    terms_ref, act_ref, totals_ref = refs[n_parts + 6 :]
    cols, width = out_ref.shape[1:]
    rows = act_ref.shape[1] // cols
    wide = width // 2
    store_terms(terms_ref, parts_ref, gain_ref, shift_ref, pixels)
    totals_ref[...] = jnp.zeros_like(totals_ref)

    def norm(step):
        part, first_row, _ = blocks[step]
        value = part_refs[part][first_row : first_row + rows].reshape(rows * cols, act_ref.shape[2])
        act_ref[step % 2] = jnp.maximum(value * terms_ref[0:1] + terms_ref[1:2], 0.0).astype(
            jnp.bfloat16
        )

    norm(0)
    for step, (_, _, spans) in enumerate(blocks):
        if step + 1 < len(blocks):
            norm(step + 1)
        for first_lane in range(0, width, wide):
            lanes = slice(first_lane, first_lane + wide)
            result = jnp.dot(
                act_ref[step % 2], weight_ref[:, lanes], preferred_element_type=jnp.float32
            )
            placed = result.reshape(rows, cols, wide)
            done = 0
            for out_row, count in spans:
                out_ref[out_row : out_row + count, :, lanes] = placed[done : done + count]
                done += count
            totals_ref[0, :, lanes] += summed_rows(result)
            totals_ref[1, :, lanes] += summed_rows(result * result)
    store_sums(sums_ref, slice(None), totals_ref[0], totals_ref[1])


def outer_project_body(pixels, u_ref, parts_ref, gain_ref, shift_ref, weight_ref, out_ref, terms_ref, act_ref):
    count, cols, width = out_ref.shape
    wide = width // 2
    store_terms(terms_ref, parts_ref, gain_ref, shift_ref, pixels)
    value = u_ref[...].reshape(count * cols, u_ref.shape[2])
    act_ref[...] = jnp.maximum(value * terms_ref[0:1] + terms_ref[1:2], 0.0).astype(jnp.bfloat16)

    for first_lane in range(0, width, wide):
        lanes = slice(first_lane, first_lane + wide)
        result = jnp.dot(act_ref[...], weight_ref[:, lanes], preferred_element_type=jnp.float32)
        out_ref[:, :, lanes] = result.reshape(count, cols, wide)


def last_body(pixels, u_ref, parts_ref, gain_ref, shift_ref, out_hbm, terms_ref, rows_ref, sent):
    store_terms(terms_ref, parts_ref, gain_ref, shift_ref, pixels)

    def piece(row):
        return pltpu.make_async_copy(rows_ref.at[row], out_hbm.at[0, row], sent.at[row])

    @pl.loop(0, u_ref.shape[0])
    def _(row):
        value = u_ref[row] * terms_ref[0:1] + terms_ref[1:2]
        rows_ref[row] = jnp.maximum(value, 0.0).astype(jnp.bfloat16)
        piece(row).start()

    @pl.loop(0, u_ref.shape[0])
    def _(row):
        piece(row).wait()


def dilated_inner(x, taps, weight):
    rows, cols, depth = x.shape[1:]
    inner = rows - 2 * RATE
    return pl.pallas_call(
        inner_body,
        out_shape=[
            pltpu.VMEM((inner, cols, depth), jnp.float32),
            pltpu.VMEM((2, depth), jnp.float32),
            pltpu.VMEM((rows, cols, depth), x.dtype),
            pltpu.VMEM(taps.shape, taps.dtype),
            pltpu.VMEM(weight.shape, weight.dtype),
        ],
        in_specs=[HBM] * 3,
        out_specs=[VMEM] * 5,
        scratch_shapes=[pltpu.SemaphoreType.DMA((4,))] + [pltpu.SemaphoreType.DMA] * 2,
        compiler_params=pltpu.CompilerParams(vmem_limit_bytes=12 << 20),
        cost_estimate=pl.CostEstimate(
            flops=20 * inner * cols * depth, bytes_accessed=6 * rows * cols * depth, transcendentals=0
        ),
    )(x, taps, weight)


def kept_in_hbm(array):
    return pltpu.with_memory_space_constraint(array, pltpu.HBM)


def edge_rows(x):
    edges = [(count,) + x.shape[2:] for count in (2 * RATE, RATE, RATE)]
    return pl.pallas_call(
        load_body,
        out_shape=[pltpu.VMEM(shape, x.dtype) for shape in edges],
        in_specs=[HBM],
        out_specs=[VMEM] * 3,
        scratch_shapes=[pltpu.SemaphoreType.DMA((3,))],
        compiler_params=pltpu.CompilerParams(vmem_limit_bytes=4 << 20),
    )(x)


def dilated_edges(x, chip, near, weight, inner_sums):
    cols, depth = x.shape[1:]
    return kernel_call(
        edge_body,
        [((2 * RATE, cols, depth), jnp.float32), ((2, depth), jnp.float32)],
        5,
        12 << 20,
        flops=40 * RATE * cols * depth,
        moved=20 * RATE * cols * depth,
    )(x, chip, near, weight, inner_sums)


def project(pixels, pieces, blocks, parts, gain, shift, weight):
    rows = sum(piece.shape[0] for piece in pieces)
    cols, depth = pieces[0].shape[1:]
    width = weight.shape[1]
    outs = [((rows, cols, width), jnp.float32), ((2, width), jnp.float32)]
    return pl.pallas_call(
        functools.partial(project_body, pixels, blocks, len(pieces)),
        out_shape=[pltpu.VMEM(shape, dtype) for shape, dtype in outs],
        in_specs=[VMEM] * (len(pieces) + 4),
        out_specs=[VMEM] * len(outs),
        scratch_shapes=[
            pltpu.VMEM((2, depth), jnp.float32),
            pltpu.VMEM((2, rows // len(blocks) * cols, depth), jnp.bfloat16),
            pltpu.VMEM((2, 8, width), jnp.float32),
        ],
        compiler_params=pltpu.CompilerParams(vmem_limit_bytes=24 << 20),
        cost_estimate=pl.CostEstimate(
            flops=2 * rows * cols * depth * width,
            bytes_accessed=4 * rows * cols * (depth + width) + 2 * depth * width,
            transcendentals=0,
        ),
    )(*pieces, parts, gain, shift, weight)


def dilated_outer(x, chip, near, far, taps):
    cols, depth = x.shape[1:]
    (outer,) = kernel_call(
        outer_body,
        [((2 * RATE, cols, depth), jnp.float32)],
        5,
        8 << 20,
        flops=36 * RATE * cols * depth,
        moved=20 * RATE * cols * depth,
    )(x, chip, near, far, taps)
    return outer


def project_outer(pixels, u, parts, gain, shift, weight):
    rows, cols, depth = u.shape
    width = weight.shape[1]
    (outer,) = kernel_call(
        functools.partial(outer_project_body, pixels),
        [((rows, cols, width), jnp.float32)],
        5,
        12 << 20,
        scratch=[pltpu.VMEM((2, depth), jnp.float32), pltpu.VMEM((rows * cols, depth), jnp.bfloat16)],
        flops=2 * rows * cols * depth * width,
        moved=4 * rows * cols * (depth + width) + 2 * depth * width,
    )(u, parts, gain, shift, weight)
    return outer


def dilated_second(pixels, u, outer, parts, gain, shift, taps, weight):
    rows, cols, depth = u.shape
    return pl.pallas_call(
        functools.partial(third_body, pixels),
        out_shape=[
            pltpu.VMEM((rows, cols, depth), jnp.float32),
            pltpu.VMEM((2, depth), jnp.float32),
            pltpu.VMEM(weight.shape, weight.dtype),
        ],
        in_specs=[VMEM] * 6 + [HBM],
        out_specs=[VMEM] * 3,
        scratch_shapes=[
            pltpu.VMEM((2, depth), jnp.float32),
            pltpu.VMEM((rows + 2 * RATE, cols + 2 * PAD, LANES), jnp.float32),
            pltpu.SemaphoreType.DMA,
        ],
        compiler_params=pltpu.CompilerParams(vmem_limit_bytes=16 << 20),
        cost_estimate=pl.CostEstimate(
            flops=26 * rows * cols * depth, bytes_accessed=8 * rows * cols * depth, transcendentals=0
        ),
    )(u, outer, parts, gain, shift, taps, weight)


def last_norm(pixels, u, parts, gain, shift):
    rows, cols, depth = u.shape
    return pl.pallas_call(
        functools.partial(last_body, pixels),
        out_shape=jax.ShapeDtypeStruct((1, rows, cols, depth), jnp.bfloat16),
        in_specs=[VMEM] * 4,
        out_specs=HBM,
        scratch_shapes=[
            pltpu.VMEM((2, depth), jnp.float32),
            pltpu.VMEM((rows, cols, depth), jnp.bfloat16),
            pltpu.SemaphoreType.DMA((rows,)),
        ],
        compiler_params=pltpu.CompilerParams(vmem_limit_bytes=16 << 20),
        cost_estimate=pl.CostEstimate(
            flops=3 * rows * cols * depth, bytes_accessed=6 * rows * cols * depth, transcendentals=0
        ),
    )(u, parts, gain, shift)


def pair_body(own_ref, other_ref, out_ref):
    out_ref[...] = jnp.broadcast_to((own_ref[...] + other_ref[...])[None], out_ref.shape)


def group_body(parts_ref, out_ref):
    out_ref[...] = jnp.broadcast_to(jnp.sum(parts_ref[...], axis=0)[None], out_ref.shape)


def gathered_sums(value, beside=None):
    plane, line = ("batch_1", "space_0"), ("batch_0",)
    other = lax.ppermute(value, "space_1", [(0, 1), (1, 0)])
    if beside is not None:
        other, beside = lax.optimization_barrier((other, beside))
    shape = (lax.axis_size(plane),) + value.shape
    (copies,) = kernel_call(pair_body, [(shape, jnp.float32)], 2, 2 << 20)(value, other)
    parts = lax.all_to_all(copies, plane, 0, 0)
    shape = (lax.axis_size(line),) + value.shape
    (copies,) = kernel_call(group_body, [(shape, jnp.float32)], 1, 2 << 20)(parts)
    return lax.all_to_all(copies, line, 0, 0), beside


def from_neighbours(chip, near, far):
    ends = [pair for i in range(1, lax.axis_size(SPACE) - 1, 2) for pair in ((i, i + 1), (i + 1, i))]
    near = lax.ppermute(near, SPACE, ends)
    chip = lax.ppermute(chip, "space_1", [(0, 1), (1, 0)])
    return chip, near, lax.ppermute(far, SPACE, ends)


def per_device(
    features,
    depth_one,
    gain_one,
    shift_one,
    point_one,
    gain_two,
    shift_two,
    depth_two,
    gain_three,
    shift_three,
    point_two,
    gain_four,
    shift_four,
):
    rows, cols = features.shape[1:3]
    pixels = rows * cols * lax.axis_size(BATCH) * lax.axis_size(SPACE)
    names = (gain_one, shift_one, gain_two, shift_two, gain_three, shift_three, gain_four, shift_four)
    terms = [term.reshape(-1, LANES) for term in names]
    features = kept_in_hbm(features)
    chip, near, far = from_neighbours(*edge_rows(features))
    step = 2 * RATE
    in_order = [(0, row, [(row, step)]) for row in range(0, rows, step)]
    edges_first = [(0, 0, [(0, RATE), (rows - RATE, RATE)])]
    edges_first += [(1, row, [(row + RATE, step)]) for row in range(0, rows - step, step)]
    inner, inner_sums, x, taps, weight = dilated_inner(
        features, kept_in_hbm(depth_one), kept_in_hbm(point_one)
    )
    edges, sums = dilated_edges(x, chip, near, taps, inner_sums)
    parts, outer = gathered_sums(sums, dilated_outer(x, chip, near, far, taps))
    second, sums = project(pixels, (edges, inner), edges_first, parts, *terms[0:2], weight)
    outer = project_outer(pixels, outer, parts, *terms[0:2], weight)
    parts, outer = gathered_sums(sums, outer)
    third, sums, weight = dilated_second(
        pixels, second, outer, parts, *terms[2:4], depth_two, kept_in_hbm(point_two)
    )
    parts, _ = gathered_sums(sums)
    fourth, sums = project(pixels, (third,), in_order, parts, *terms[4:6], weight)
    parts, _ = gathered_sums(sums)
    return last_norm(pixels, fourth, parts, *terms[6:8])


def solution(mesh):
    finer = Mesh(mesh.devices.reshape(8, 4, 4, 2), ("batch_0", "batch_1", "space_0", "space_1"))
    placed = (P(BATCH, SPACE, None, None),) + (P(),) * 12
    return jax.shard_map(
        per_device,
        mesh=finer,
        in_specs=placed,
        out_specs=P(BATCH, SPACE, None, None),
        check_vma=False,
    )
```

```python
import functools

import jax
import jax.numpy as jnp
from jax import lax
from jax.experimental import pallas as pl
from jax.experimental.pallas import tpu as pltpu
from jax.sharding import Mesh
from jax.sharding import PartitionSpec as P

RATE = 2
LANES = 128
PAD = 8
BATCH = ("batch_0", "batch_1")
SPACE = ("space_0", "space_1")

epsilon = 1e-05

VMEM = pl.BlockSpec(memory_space=pltpu.VMEM)
HBM = pl.BlockSpec(memory_space=pltpu.HBM)


def kernel_call(body, outs, n_in, limit, scratch=(), flops=0, moved=0):
    return pl.pallas_call(
        body,
        out_shape=[pltpu.VMEM(shape, dtype) for shape, dtype in outs],
        in_specs=[VMEM] * n_in,
        out_specs=[VMEM] * len(outs),
        scratch_shapes=list(scratch),
        compiler_params=pltpu.CompilerParams(vmem_limit_bytes=limit),
        cost_estimate=pl.CostEstimate(flops=flops, bytes_accessed=moved, transcendentals=0),
    )


def moved_down(row):
    gap = jnp.zeros((RATE, row.shape[1]), row.dtype)
    return jnp.concatenate([gap, row[: row.shape[0] - RATE]], axis=0)


def moved_up(row):
    gap = jnp.zeros((RATE, row.shape[1]), row.dtype)
    return jnp.concatenate([row[RATE:], gap], axis=0)


def taps_of(filter_ref, lanes):
    return [filter_ref[tap, :, lanes].astype(jnp.float32) for tap in range(3)]


def dilated_row(rows, taps):
    sides = []
    for tap_col in range(3):
        side = None
        for tap_row in range(3):
            term = rows[tap_row] * taps[tap_row][tap_col : tap_col + 1]
            side = term if side is None else side + term
        sides.append(side)
    return sides[1] + moved_down(sides[0]) + moved_up(sides[2])


def summed_rows(value):
    return jnp.sum(value.reshape(value.shape[0] // 8, 8, value.shape[1]), axis=0)


def store_sums(sums_ref, lanes, total, squares):
    sums_ref[0:1, lanes] = jnp.sum(total, axis=0, keepdims=True)
    sums_ref[1:2, lanes] = jnp.sum(squares, axis=0, keepdims=True)


def dilated_rows(row_at, rows, taps, out_ref, lanes):
    total = squares = None
    for place, row in sorted(enumerate(rows), key=lambda pair: (pair[1] % 2, pair[1])):
        value = dilated_row([row_at(row - RATE), row_at(row), row_at(row + RATE)], taps)
        out_ref[place, :, lanes] = value
        part, part_squares = summed_rows(value), summed_rows(value * value)
        total = part if total is None else total + part
        squares = part_squares if squares is None else squares + part_squares
    return total, squares


def inner_body(
    x_hbm, filter_hbm, weight_hbm, out_ref, sums_ref, x_ref, filter_ref, weight_ref, arrived,
    filter_arrived, weight_arrived,
):
    count, _, depth = x_ref.shape
    wide = depth // arrived.shape[0]

    def piece(place):
        lanes = pl.ds(place * wide, wide)
        return pltpu.make_async_copy(
            x_hbm.at[0, :, :, lanes], x_ref.at[:, :, lanes], arrived.at[place]
        )

    taps_copy = pltpu.make_async_copy(filter_hbm, filter_ref, filter_arrived)
    taps_copy.start()
    for place in range(arrived.shape[0]):
        piece(place).start()
    weight_copy = pltpu.make_async_copy(weight_hbm, weight_ref, weight_arrived)
    weight_copy.start()
    taps_copy.wait()
    for place in range(arrived.shape[0]):
        piece(place).wait()

        @pl.loop(place * wide // LANES, (place + 1) * wide // LANES, unroll=2)
        def _(block):
            lanes = pl.ds(pl.multiple_of(block * LANES, LANES), LANES)
            total, squares = dilated_rows(
                functools.cache(lambda row: x_ref[row, :, lanes].astype(jnp.float32)),
                range(RATE, count - RATE),
                taps_of(filter_ref, lanes),
                out_ref,
                lanes,
            )
            store_sums(sums_ref, lanes, total, squares)

    weight_copy.wait()


def edge_starts(count):
    core = lax.axis_index("space_1")
    return (
        (1 - core) * (count - 2 * RATE),
        core * (count - RATE),
        RATE + core * (count - 3 * RATE),
    )


def load_body(x_hbm, chip_ref, near_ref, far_ref, arrived):
    starts = edge_starts(x_hbm.shape[1])
    copies = [
        pltpu.make_async_copy(
            x_hbm.at[0, pl.ds(start, out_ref.shape[0])], out_ref, arrived.at[place]
        )
        for place, (start, out_ref) in enumerate(zip(starts, (chip_ref, near_ref, far_ref)))
    ]
    for copy in copies:
        copy.start()
    for copy in copies:
        copy.wait()


def halo_row(chip_ref, near_ref, far_ref, row, count, lanes):
    core = lax.axis_index("space_1")
    if row < 0:
        chip_holds, chip_row = core == 1, row + 2 * RATE
        cross_ref, cross_row = (near_ref, row + RATE) if row >= -RATE else (far_ref, row + 2 * RATE)
    else:
        chip_holds, chip_row = core == 0, row - count
        cross_ref, cross_row = (
            (near_ref, row - count) if row < count + RATE else (far_ref, row - count - RATE)
        )
    value = jnp.where(chip_holds, chip_ref[chip_row, :, lanes], cross_ref[cross_row, :, lanes])
    return value.astype(jnp.float32)


def edge_body(x_ref, chip_ref, near_ref, filter_ref, inner_ref, out_ref, sums_ref):
    count = x_ref.shape[0]

    @pl.loop(0, x_ref.shape[2] // LANES, unroll=2)
    def _(block):
        lanes = pl.ds(pl.multiple_of(block * LANES, LANES), LANES)

        @functools.cache
        def row_at(row):
            if 0 <= row < count:
                return x_ref[row, :, lanes].astype(jnp.float32)
            return halo_row(chip_ref, near_ref, None, row, count, lanes)

        rows = (*range(RATE), *range(count - RATE, count))
        total, squares = dilated_rows(row_at, rows, taps_of(filter_ref, lanes), out_ref, lanes)
        store_sums(sums_ref, lanes, total, squares)
        sums_ref[:, lanes] = sums_ref[:, lanes] + inner_ref[:, lanes]


def outer_body(x_ref, chip_ref, near_ref, far_ref, filter_ref, out_ref):
    count = x_ref.shape[0]

    @pl.loop(0, x_ref.shape[2] // LANES, unroll=2)
    def _(block):
        lanes = pl.ds(pl.multiple_of(block * LANES, LANES), LANES)
        taps = taps_of(filter_ref, lanes)

        @functools.cache
        def row_at(row):
            if 0 <= row < count:
                return x_ref[row, :, lanes].astype(jnp.float32)
            return halo_row(chip_ref, near_ref, far_ref, row, count, lanes)

        for place, row in enumerate((*range(-RATE, 0), *range(count, count + RATE))):
            rows = [row_at(row - RATE), row_at(row), row_at(row + RATE)]
            out_ref[place, :, lanes] = dilated_row(rows, taps)


def store_terms(terms_ref, parts_ref, gain_ref, shift_ref, pixels):
    for block in range(gain_ref.shape[0]):
        lanes = slice(block * LANES, (block + 1) * LANES)
        sums = jnp.sum(parts_ref[:, :, lanes], axis=0)
        average = sums[0:1] / pixels
        variance = sums[1:2] / pixels - average * average
        factor = gain_ref[block : block + 1] * lax.rsqrt(variance + epsilon)
        terms_ref[0:1, lanes] = factor
        terms_ref[1:2, lanes] = shift_ref[block : block + 1] - average * factor


def third_body(
    pixels, u_ref, outer_ref, parts_ref, gain_ref, shift_ref, filter_ref,
    weight_hbm, out_ref, sums_ref, weight_ref, terms_ref, padded_ref, arrived,
):
    count = u_ref.shape[0]
    weight_copy = pltpu.make_async_copy(weight_hbm, weight_ref, arrived)
    weight_copy.start()
    store_terms(terms_ref, parts_ref, gain_ref, shift_ref, pixels)
    cols = u_ref.shape[1]
    gap = jnp.zeros((count + 2 * RATE, PAD, LANES), jnp.float32)
    padded_ref[:, :PAD] = gap
    padded_ref[:, PAD + cols :] = gap

    @pl.loop(0, u_ref.shape[2] // LANES, unroll=2)
    def _(block):
        lanes = pl.ds(pl.multiple_of(block * LANES, LANES), LANES)
        taps = taps_of(filter_ref, lanes)
        factor = terms_ref[0:1, lanes]
        offset = terms_ref[1:2, lanes]
        strip = lax.axis_index(SPACE)
        above = (strip > 0).astype(jnp.float32)
        below = (strip < lax.axis_size(SPACE) - 1).astype(jnp.float32)

        def row_at(row):
            if row < 0:
                value = outer_ref[row + RATE, :, lanes]
                value = value * (factor * above) + offset * above
            elif row >= count:
                value = outer_ref[row - count + RATE, :, lanes]
                value = value * (factor * below) + offset * below
            else:
                value = u_ref[row, :, lanes] * factor + offset
            return jnp.maximum(value, 0.0).astype(jnp.bfloat16).astype(jnp.float32)

        for row in range(-RATE, count + RATE):
            padded_ref[row + RATE, PAD : PAD + cols] = row_at(row)
        total = squares = 0.0
        for row in range(count):
            value = None
            for tap_row in range(3):
                for tap_col in range(3):
                    first_col = PAD + (tap_col - 1) * RATE
                    term = padded_ref[row + tap_row * RATE, first_col : first_col + cols]
                    term = term * taps[tap_row][tap_col : tap_col + 1]
                    value = term if value is None else value + term
            out_ref[row, :, lanes] = value
            total = total + summed_rows(value)
            squares = squares + summed_rows(value * value)
        store_sums(sums_ref, lanes, total, squares)

    weight_copy.wait()


def project_body(pixels, blocks, n_parts, *refs):
    part_refs = refs[:n_parts]
    parts_ref, gain_ref, shift_ref, weight_ref, out_ref, sums_ref = refs[n_parts : n_parts + 6]
    terms_ref, act_ref, totals_ref = refs[n_parts + 6 :]
    cols, width = out_ref.shape[1:]
    rows = act_ref.shape[1] // cols
    wide = width // 2
    store_terms(terms_ref, parts_ref, gain_ref, shift_ref, pixels)
    totals_ref[...] = jnp.zeros_like(totals_ref)

    def norm(step):
        part, first_row, _ = blocks[step]
        value = part_refs[part][first_row : first_row + rows].reshape(rows * cols, act_ref.shape[2])
        act_ref[step % 2] = jnp.maximum(value * terms_ref[0:1] + terms_ref[1:2], 0.0).astype(
            jnp.bfloat16
        )

    norm(0)
    for step, (_, _, spans) in enumerate(blocks):
        if step + 1 < len(blocks):
            norm(step + 1)
        for first_lane in range(0, width, wide):
            lanes = slice(first_lane, first_lane + wide)
            result = jnp.dot(
                act_ref[step % 2], weight_ref[:, lanes], preferred_element_type=jnp.float32
            )
            placed = result.reshape(rows, cols, wide)
            done = 0
            for out_row, count in spans:
                out_ref[out_row : out_row + count, :, lanes] = placed[done : done + count]
                done += count
            totals_ref[0, :, lanes] += summed_rows(result)
            totals_ref[1, :, lanes] += summed_rows(result * result)
    store_sums(sums_ref, slice(None), totals_ref[0], totals_ref[1])


def outer_project_body(pixels, u_ref, parts_ref, gain_ref, shift_ref, weight_ref, out_ref, terms_ref, act_ref):
    count, cols, width = out_ref.shape
    wide = width // 2
    store_terms(terms_ref, parts_ref, gain_ref, shift_ref, pixels)
    value = u_ref[...].reshape(count * cols, u_ref.shape[2])
    act_ref[...] = jnp.maximum(value * terms_ref[0:1] + terms_ref[1:2], 0.0).astype(jnp.bfloat16)

    for first_lane in range(0, width, wide):
        lanes = slice(first_lane, first_lane + wide)
        result = jnp.dot(act_ref[...], weight_ref[:, lanes], preferred_element_type=jnp.float32)
        out_ref[:, :, lanes] = result.reshape(count, cols, wide)


def last_body(pixels, u_ref, parts_ref, gain_ref, shift_ref, out_hbm, terms_ref, rows_ref, sent):
    store_terms(terms_ref, parts_ref, gain_ref, shift_ref, pixels)

    def piece(row):
        return pltpu.make_async_copy(rows_ref.at[row], out_hbm.at[0, row], sent.at[row])

    @pl.loop(0, u_ref.shape[0], unroll=3)
    def _(row):
        value = u_ref[row] * terms_ref[0:1] + terms_ref[1:2]
        rows_ref[row] = jnp.maximum(value, 0.0).astype(jnp.bfloat16)
        piece(row).start()

    @pl.loop(0, u_ref.shape[0])
    def _(row):
        piece(row).wait()


def dilated_inner(x, taps, weight):
    rows, cols, depth = x.shape[1:]
    inner = rows - 2 * RATE
    return pl.pallas_call(
        inner_body,
        out_shape=[
            pltpu.VMEM((inner, cols, depth), jnp.float32),
            pltpu.VMEM((2, depth), jnp.float32),
            pltpu.VMEM((rows, cols, depth), x.dtype),
            pltpu.VMEM(taps.shape, taps.dtype),
            pltpu.VMEM(weight.shape, weight.dtype),
        ],
        in_specs=[HBM] * 3,
        out_specs=[VMEM] * 5,
        scratch_shapes=[pltpu.SemaphoreType.DMA((4,))] + [pltpu.SemaphoreType.DMA] * 2,
        compiler_params=pltpu.CompilerParams(vmem_limit_bytes=12 << 20),
        cost_estimate=pl.CostEstimate(
            flops=20 * inner * cols * depth, bytes_accessed=6 * rows * cols * depth, transcendentals=0
        ),
    )(x, taps, weight)


def kept_in_hbm(array):
    return pltpu.with_memory_space_constraint(array, pltpu.HBM)


def edge_rows(x):
    edges = [(count,) + x.shape[2:] for count in (2 * RATE, RATE, RATE)]
    return pl.pallas_call(
        load_body,
        out_shape=[pltpu.VMEM(shape, x.dtype) for shape in edges],
        in_specs=[HBM],
        out_specs=[VMEM] * 3,
        scratch_shapes=[pltpu.SemaphoreType.DMA((3,))],
        compiler_params=pltpu.CompilerParams(vmem_limit_bytes=4 << 20),
    )(x)


def dilated_edges(x, chip, near, weight, inner_sums):
    cols, depth = x.shape[1:]
    return kernel_call(
        edge_body,
        [((2 * RATE, cols, depth), jnp.float32), ((2, depth), jnp.float32)],
        5,
        12 << 20,
        flops=40 * RATE * cols * depth,
        moved=20 * RATE * cols * depth,
    )(x, chip, near, weight, inner_sums)


def project(pixels, pieces, blocks, parts, gain, shift, weight):
    rows = sum(piece.shape[0] for piece in pieces)
    cols, depth = pieces[0].shape[1:]
    width = weight.shape[1]
    outs = [((rows, cols, width), jnp.float32), ((2, width), jnp.float32)]
    return pl.pallas_call(
        functools.partial(project_body, pixels, blocks, len(pieces)),
        out_shape=[pltpu.VMEM(shape, dtype) for shape, dtype in outs],
        in_specs=[VMEM] * (len(pieces) + 4),
        out_specs=[VMEM] * len(outs),
        scratch_shapes=[
            pltpu.VMEM((2, depth), jnp.float32),
            pltpu.VMEM((2, rows // len(blocks) * cols, depth), jnp.bfloat16),
            pltpu.VMEM((2, 8, width), jnp.float32),
        ],
        compiler_params=pltpu.CompilerParams(vmem_limit_bytes=24 << 20),
        cost_estimate=pl.CostEstimate(
            flops=2 * rows * cols * depth * width,
            bytes_accessed=4 * rows * cols * (depth + width) + 2 * depth * width,
            transcendentals=0,
        ),
    )(*pieces, parts, gain, shift, weight)


def dilated_outer(x, chip, near, far, taps):
    cols, depth = x.shape[1:]
    (outer,) = kernel_call(
        outer_body,
        [((2 * RATE, cols, depth), jnp.float32)],
        5,
        8 << 20,
        flops=36 * RATE * cols * depth,
        moved=20 * RATE * cols * depth,
    )(x, chip, near, far, taps)
    return outer


def project_outer(pixels, u, parts, gain, shift, weight):
    rows, cols, depth = u.shape
    width = weight.shape[1]
    (outer,) = kernel_call(
        functools.partial(outer_project_body, pixels),
        [((rows, cols, width), jnp.float32)],
        5,
        12 << 20,
        scratch=[pltpu.VMEM((2, depth), jnp.float32), pltpu.VMEM((rows * cols, depth), jnp.bfloat16)],
        flops=2 * rows * cols * depth * width,
        moved=4 * rows * cols * (depth + width) + 2 * depth * width,
    )(u, parts, gain, shift, weight)
    return outer


def dilated_second(pixels, u, outer, parts, gain, shift, taps, weight):
    rows, cols, depth = u.shape
    return pl.pallas_call(
        functools.partial(third_body, pixels),
        out_shape=[
            pltpu.VMEM((rows, cols, depth), jnp.float32),
            pltpu.VMEM((2, depth), jnp.float32),
            pltpu.VMEM(weight.shape, weight.dtype),
        ],
        in_specs=[VMEM] * 6 + [HBM],
        out_specs=[VMEM] * 3,
        scratch_shapes=[
            pltpu.VMEM((2, depth), jnp.float32),
            pltpu.VMEM((rows + 2 * RATE, cols + 2 * PAD, LANES), jnp.float32),
            pltpu.SemaphoreType.DMA,
        ],
        compiler_params=pltpu.CompilerParams(vmem_limit_bytes=16 << 20),
        cost_estimate=pl.CostEstimate(
            flops=26 * rows * cols * depth, bytes_accessed=8 * rows * cols * depth, transcendentals=0
        ),
    )(u, outer, parts, gain, shift, taps, weight)


def last_norm(pixels, u, parts, gain, shift):
    rows, cols, depth = u.shape
    return pl.pallas_call(
        functools.partial(last_body, pixels),
        out_shape=jax.ShapeDtypeStruct((1, rows, cols, depth), jnp.bfloat16),
        in_specs=[VMEM] * 4,
        out_specs=HBM,
        scratch_shapes=[
            pltpu.VMEM((2, depth), jnp.float32),
            pltpu.VMEM((rows, cols, depth), jnp.bfloat16),
            pltpu.SemaphoreType.DMA((rows,)),
        ],
        compiler_params=pltpu.CompilerParams(vmem_limit_bytes=16 << 20),
        cost_estimate=pl.CostEstimate(
            flops=3 * rows * cols * depth, bytes_accessed=6 * rows * cols * depth, transcendentals=0
        ),
    )(u, parts, gain, shift)


def pair_body(own_ref, other_ref, out_ref):
    out_ref[...] = jnp.broadcast_to((own_ref[...] + other_ref[...])[None], out_ref.shape)


def group_body(parts_ref, out_ref):
    out_ref[...] = jnp.broadcast_to(jnp.sum(parts_ref[...], axis=0)[None], out_ref.shape)


def gathered_sums(value, beside=None):
    plane, line = ("batch_1", "space_0"), ("batch_0",)
    other = lax.ppermute(value, "space_1", [(0, 1), (1, 0)])
    if beside is not None:
        other, beside = lax.optimization_barrier((other, beside))
    shape = (lax.axis_size(plane),) + value.shape
    (copies,) = kernel_call(pair_body, [(shape, jnp.float32)], 2, 2 << 20)(value, other)
    parts = lax.all_to_all(copies, plane, 0, 0)
    shape = (lax.axis_size(line),) + value.shape
    (copies,) = kernel_call(group_body, [(shape, jnp.float32)], 1, 2 << 20)(parts)
    return lax.all_to_all(copies, line, 0, 0), beside


def from_neighbours(chip, near, far):
    ends = [pair for i in range(1, lax.axis_size(SPACE) - 1, 2) for pair in ((i, i + 1), (i + 1, i))]
    near = lax.ppermute(near, SPACE, ends)
    chip = lax.ppermute(chip, "space_1", [(0, 1), (1, 0)])
    return chip, near, lax.ppermute(far, SPACE, ends)


def per_device(
    features,
    depth_one,
    gain_one,
    shift_one,
    point_one,
    gain_two,
    shift_two,
    depth_two,
    gain_three,
    shift_three,
    point_two,
    gain_four,
    shift_four,
):
    rows, cols = features.shape[1:3]
    pixels = rows * cols * lax.axis_size(BATCH) * lax.axis_size(SPACE)
    names = (gain_one, shift_one, gain_two, shift_two, gain_three, shift_three, gain_four, shift_four)
    terms = [term.reshape(-1, LANES) for term in names]
    features = kept_in_hbm(features)
    chip, near, far = from_neighbours(*edge_rows(features))
    step = 2 * RATE
    in_order = [(0, row, [(row, step)]) for row in range(0, rows, step)]
    edges_first = [(0, 0, [(0, RATE), (rows - RATE, RATE)])]
    edges_first += [(1, row, [(row + RATE, step)]) for row in range(0, rows - step, step)]
    inner, inner_sums, x, taps, weight = dilated_inner(
        features, kept_in_hbm(depth_one), kept_in_hbm(point_one)
    )
    edges, sums = dilated_edges(x, chip, near, taps, inner_sums)
    parts, outer = gathered_sums(sums, dilated_outer(x, chip, near, far, taps))
    second, sums = project(pixels, (edges, inner), edges_first, parts, *terms[0:2], weight)
    outer = project_outer(pixels, outer, parts, *terms[0:2], weight)
    parts, outer = gathered_sums(sums, outer)
    third, sums, weight = dilated_second(
        pixels, second, outer, parts, *terms[2:4], depth_two, kept_in_hbm(point_two)
    )
    parts, _ = gathered_sums(sums)
    fourth, sums = project(pixels, (third,), in_order, parts, *terms[4:6], weight)
    parts, _ = gathered_sums(sums)
    return last_norm(pixels, fourth, parts, *terms[6:8])


def solution(mesh):
    finer = Mesh(mesh.devices.reshape(8, 4, 4, 2), ("batch_0", "batch_1", "space_0", "space_1"))
    placed = (P(BATCH, SPACE, None, None),) + (P(),) * 12
    return jax.shard_map(
        per_device,
        mesh=finer,
        in_specs=placed,
        out_specs=P(BATCH, SPACE, None, None),
        check_vma=False,
    )
```
